128 devices in a mesh: seq: 32 (over x, z, core), head: 4 (over y).
Axes of the slice: x: 4, y: 4, z: 4, core: 2. Of those that a mesh axis runs over, the one named last changes fastest.
Arguments:
- queries: bfloat16 [16384, 5120], P('seq', 'head'), may hold values from -13 to 13, as said below
- keys: bfloat16 [16384, 1024], P('seq', 'head'), may hold values from -13 to 13, as said below
- values: bfloat16 [16384, 1024], P('seq', 'head'), may hold values from -6 to 6
- out_weight: bfloat16 [5120, 2560], P('head', 'seq'), may hold values from -0.078125 to 0.078125
- d_proj: bfloat16 [16384, 2560], P('seq', 'head'), may hold values from -6 to 6
- block_section: int32 [128], replicated, may hold values from 0 to 15, as said below
- section_parent: int32 [16], replicated, may hold values from -1 to 14, as said below
- xref_owner: int32 [1536, 1], P('seq'), may hold values from 0 to 31; in each aligned block of 48 rows (0 to 47, 48 to 95, ...) at most 2 rows name the same one
- xref_block: int32 [128, 12], P('seq'), may hold values from 0 to 3
- xref_valid: int32 [128, 12], P('seq'), may hold values 0 or 1
Outputs:
- projected: bfloat16 [16384, 2560], P('seq', 'head')
- d_queries: bfloat16 [16384, 5120], P('seq', 'head')
- d_keys: bfloat16 [16384, 1024], P('seq', 'head')
- d_values: bfloat16 [16384, 1024], P('seq', 'head')
The draws below stay inside these ranges and needn't reach their ends.
Inputs may be any that keep to these rules, and one draw needn't show every extreme that they name: `queries`: entries of order one; a few rows of larger norm. `keys`: entries of order one; a few rows of larger norm. section_parent[s] is an earlier section for s > 0, and section_parent[0] = -1. `block_section`: sections are runs of consecutive blocks, 2 to 14 blocks each, some section exactly 14; no section begins at a block whose index is a positive multiple of 4. `xref_owner`: among the 48 rows of one device, no owner is named more than 2 times; some owner exactly 2 times.
All inputs are finite; a program needn't handle non-finite values. No bound on the sum of `xref_valid` on one device may be relied on, other than what follows from the above.
Results may differ from the reference program's by a relative error of at most 0.015.
The reference program's roundings to bfloat16 on the way count: a program that leaves them out, or rounds other values in their place, can miss the bound.
Values may be sent and summed in bfloat16 or wider, within the bound.
A program may use at most 192 MiB of HBM per device.

```python
import math
import jax
import jax.numpy as jnp
import numpy as np
from jax import lax

QUERY_HEAD_COUNT = 40
KEY_VALUE_HEADS = 8
HEAD_DIMENSION = 128
OUTW = 2560
BLK = 128
LOOK = 4
ANC = 2
XREF = 12
BPD = 4
BLOCKS = 128
DOCUMENT_TOKENS = 16384
SECTIONS = 16
CAP = 2
N_SEQ = 32


def draw_queries(key, part):
    dimension_list = (DOCUMENT_TOKENS, QUERY_HEAD_COUNT * HEAD_DIMENSION)
    values_f = jax.random.truncated_normal(jax.random.fold_in(key, 1), -4.5, 4.5, dimension_list, jnp.float32)
    return values_f.astype(jnp.bfloat16)


def draw_keys(key, part):
    dimension_list = (DOCUMENT_TOKENS, KEY_VALUE_HEADS * HEAD_DIMENSION)
    values_f = jax.random.truncated_normal(jax.random.fold_in(key, 2), -4.5, 4.5, dimension_list, jnp.float32)
    return values_f.astype(jnp.bfloat16)


def draw_block_section(key, part):
    offset_table = jnp.array([-3, -2, -1, 1, 2, 3], jnp.int32)
    bound_ids = jnp.arange(SECTIONS - 1, dtype=jnp.int32)
    picked = jax.random.randint(jax.random.fold_in(key, 21), (SECTIONS - 1,), 0, 6, dtype=jnp.int32)
    offsets = jnp.sum(jnp.where(picked[:, None] == jnp.arange(6, dtype=jnp.int32)[None, :], offset_table[None, :], 0), axis=1)
    longest = jax.random.randint(jax.random.fold_in(key, 22), (), 0, SECTIONS - 2, dtype=jnp.int32)
    offsets = jnp.where(bound_ids == longest, -3, jnp.where(bound_ids == longest + 1, 3, offsets))
    starts = 8 * (bound_ids + 1) + offsets
    block_ids = jnp.arange(BLOCKS, dtype=jnp.int32)
    return jnp.sum((block_ids[:, None] >= starts[None, :]).astype(jnp.int32), axis=1).astype(jnp.int32)


def draw_section_parent(key, part):
    section_ids = jnp.arange(SECTIONS, dtype=jnp.int32)
    chosen = jax.random.randint(jax.random.fold_in(key, 5), (SECTIONS,), 0, jnp.maximum(section_ids, 1), dtype=jnp.int32)
    chosen = jnp.where(section_ids == SECTIONS - 1, SECTIONS - 2, chosen)
    return jnp.where(section_ids == 0, -1, chosen).astype(jnp.int32)


def plant(values, key, low, largest):
    longest = values.shape.index(max(values.shape))
    spots = []
    for shift in (0, 1):
        where = [jax.random.randint(jax.random.fold_in(key, axis), (), 0, length) for axis, length in enumerate(values.shape)]
        where[longest] = (where[longest] + shift) % values.shape[longest]
        spots.append(tuple(where))
    return values.at[spots[0]].set(low).at[spots[1]].set(largest)


def levels(stream_key, extent, pieces, smallest, top_value):
    factor_of, own = 1.0, jax.random.fold_in(stream_key, 6)
    for dim, blocks in pieces:
        draws = jnp.exp(jax.random.uniform(jax.random.fold_in(own, dim), (blocks,), jnp.float32, smallest / len(pieces), top_value / len(pieces)))
        factor_of = factor_of * jnp.repeat(draws, extent[dim] // blocks).reshape([-1 if axis == dim else 1 for axis in range(len(extent))])
    return factor_of


def assign_block(key, own, number, rows, count, top, most, lean):
    sequence = jax.random.permutation(key, count)
    heavy_load, ordinary = load_shares(count, rows * top, most, lean, True), load_shares(count, rows * top, most, lean, False)
    places = jnp.arange(count)

    def named(lengths, turn):
        used = int((lengths > 0).sum())
        fixed = max(1, used // 4)
        passed = fixed + (places - fixed + turn * (used - fixed)) % max(1, count - fixed)
        return jnp.zeros((count,), jnp.int32).at[sequence[jnp.where(places < fixed, places, passed)]].set(jnp.asarray(lengths, jnp.int32))

    lengths = jnp.where(number % 4 == 0, named(heavy_load, number // 4), named(ordinary, number - number // 4 - 1))
    mixed = jax.random.permutation(jax.random.fold_in(own, 3), count)
    giver, taker = mixed[0:count // 2 * 2:2], mixed[1:count // 2 * 2:2]
    slack = jnp.minimum(lengths[giver] - 1, most - lengths[taker]) // 2
    slack = jnp.where((giver == sequence[0]) | (taker == sequence[0]) | (lengths[taker] == 0), 0, jnp.maximum(slack, 0))
    passed = jax.random.randint(jax.random.fold_in(own, 4), (count // 2,), 0, 1 << 20) % (slack + 1)
    lengths = lengths.at[giver].add(-passed).at[taker].add(passed)
    items = jnp.searchsorted(jnp.cumsum(lengths), jnp.arange(rows * top), side="right").astype(jnp.int32)
    table = items.reshape(top, rows).T
    table = table[jax.random.permutation(jax.random.fold_in(own, 1), rows)]
    turn = jax.random.randint(jax.random.fold_in(own, 2), (rows, 1), 0, top)
    return jnp.take_along_axis(table, (jnp.arange(top)[None, :] + turn) % top, axis=1)


def load_shares(number_of, total, most, lean, full):
    portions = [(1 << 20) // math.isqrt(rank ** lean) + 1 for rank in range(1, number_of + 1)]
    largest = most if full else min(most, max(-(-total // number_of), total * portions[0] // sum(portions)))
    least = 1 if total - largest >= number_of - 1 else 0
    given, surplus = [largest] + [least] * (number_of - 1), total - largest - least * (number_of - 1)
    while surplus > 0:
        candidates = [i for i in range(1, number_of) if given[i] < largest] or [i for i in range(1, number_of) if given[i] < most]
        whole, remaining = sum([portions[i] for i in candidates]), surplus
        for i in candidates:
            more = min(most - given[i], max(1, remaining * portions[i] // whole), surplus)
            given[i] = given[i] + more
            surplus = surplus - more
    return np.array(given)


def centred(own_key, shape, deviation, reach, shards=(), held_as=jnp.bfloat16):
    drawn = deviation * jax.random.normal(own_key, shape, jnp.float32)
    if shards:
        drawn = drawn * levels(own_key, shape, shards, -0.22, 0.18)
    return jnp.clip(drawn, -reach, reach).astype(held_as)


def setup_inputs(seed: int = 0) -> dict:
    splits = jax.random.split(jax.random.key(seed), 11)
    queries = draw_queries(jax.random.fold_in(splits[10], 71), 0)
    keys = draw_keys(jax.random.fold_in(splits[10], 71), 0)
    values = centred(splits[2], (DOCUMENT_TOKENS, KEY_VALUE_HEADS * HEAD_DIMENSION), 1.0, 6.0, ((0, 32), (1, 4)))
    out_weight = centred(splits[3], (QUERY_HEAD_COUNT * HEAD_DIMENSION, OUTW), (QUERY_HEAD_COUNT * HEAD_DIMENSION) ** -0.5, 0.078125, ((0, 4), (1, 32)))
    d_proj = centred(splits[4], (DOCUMENT_TOKENS, OUTW), 1.0, 6.0, ((0, 32), (1, 4)))
    block_section = draw_block_section(jax.random.fold_in(splits[10], 71), 0)
    section_parent = draw_section_parent(jax.random.fold_in(splits[10], 71), 0)
    xref_owner_keys = jax.random.split(jax.random.fold_in(splits[7], 1), (BLOCKS * XREF) // (BPD * XREF))
    xref_owner_turns = jax.random.permutation(jax.random.fold_in(splits[7], 3), (BLOCKS * XREF) // (BPD * XREF))
    xref_owner = jax.vmap(lambda own, number: assign_block(jax.random.fold_in(splits[7], 2), own, number, BPD * XREF, N_SEQ, 1, CAP, 2))(xref_owner_keys, xref_owner_turns).reshape((BLOCKS * XREF, 1))
    xref_block = plant(jax.random.randint(splits[8], (BLOCKS, XREF), 0, BPD), jax.random.fold_in(splits[8], 1), 0, BPD - 1).astype(jnp.int32)
    xref_valid = plant((jax.random.randint(splits[9], (BLOCKS, XREF), 0, 4) < 3).astype(jnp.int32), jax.random.fold_in(splits[9], 1), 0, 1)
    return {"queries": queries, "keys": keys, "values": values, "out_weight": out_weight, "d_proj": d_proj, "block_section": block_section, "section_parent": section_parent, "xref_owner": xref_owner, "xref_block": xref_block, "xref_valid": xref_valid}


neg_large = -1e+30

def split_queries(block, kv_heads):
    row_count = block.shape[0]
    group_size = block.shape[1] // (HEAD_DIMENSION * kv_heads)
    return block.reshape(row_count, kv_heads, group_size, HEAD_DIMENSION).transpose(1, 2, 0, 3)

def merge_queries(heads):
    kv_heads, group_size, row_count, head_size = heads.shape
    return heads.transpose(2, 0, 1, 3).reshape(row_count, kv_heads * group_size * head_size)

def split_keys(key_set, kv_heads):
    num_blocks, row_count, key_value_width = key_set.shape
    return key_set.reshape(num_blocks * row_count, kv_heads, HEAD_DIMENSION).transpose(1, 0, 2)

def merge_keys(grads, num_blocks):
    kv_heads, flat_len, head_size = grads.shape
    return grads.transpose(1, 0, 2).reshape(num_blocks, flat_len // num_blocks * kv_heads * head_size)

def softmax_weights(scores, allowed):
    masked = jnp.where(allowed, scores, neg_large)
    row_max = lax.optimization_barrier(jnp.max(masked, axis=-1, keepdims=True))
    exponent = jnp.where(allowed, jnp.exp(masked - row_max), 0.0)
    return exponent / lax.optimization_barrier(jnp.sum(exponent, axis=-1, keepdims=True))

def product(form, left, right):
    return jnp.einsum(form, left.astype(jnp.float32), right.astype(jnp.float32), precision=lax.Precision.HIGHEST)

def forward_block(query_block, key_set, value_set, allowed):
    kv_heads = key_set.shape[2] // HEAD_DIMENSION
    scaling = HEAD_DIMENSION ** (-0.5)
    query_heads = split_queries(query_block, kv_heads)
    key_heads = split_keys(key_set, kv_heads)
    value_heads = split_keys(value_set, kv_heads)
    scores = product('cgqd,ckd->cgqk', query_heads, key_heads) * scaling
    weights = softmax_weights(scores, allowed[None, None])
    output = product('cgqk,ckd->cgqd', weights.astype(jnp.bfloat16), value_heads)
    return merge_queries(output).astype(jnp.bfloat16)

def backward_block(query_block, key_set, value_set, allowed, attn, d_attn):
    kv_heads = key_set.shape[2] // HEAD_DIMENSION
    scaling = HEAD_DIMENSION ** (-0.5)
    num_blocks = key_set.shape[0]
    query_heads = split_queries(query_block, kv_heads)
    key_heads = split_keys(key_set, kv_heads)
    value_heads = split_keys(value_set, kv_heads)
    scores = product('cgqd,ckd->cgqk', query_heads, key_heads) * scaling
    weights = softmax_weights(scores, allowed[None, None])
    light = weights.astype(jnp.bfloat16)
    grad_heads = split_queries(d_attn, kv_heads)
    attn_heads = split_queries(attn, kv_heads)
    delta = lax.optimization_barrier(jnp.sum(grad_heads.astype(jnp.float32) * attn_heads.astype(jnp.float32), axis=-1, keepdims=True))
    d_weights = product('cgqd,ckd->cgqk', grad_heads, value_heads)
    d_scores = (weights * (d_weights - delta) * scaling).astype(jnp.bfloat16)
    grad_query = product('cgqk,ckd->cgqd', d_scores, key_heads)
    key_terms = product('cgqk,cgqd->ckd', d_scores, query_heads)
    value_terms = product('cgqk,cgqd->ckd', light, grad_heads)
    return (merge_queries(grad_query).astype(jnp.bfloat16), merge_keys(key_terms, num_blocks), merge_keys(value_terms, num_blocks))

def reference(queries, keys, values, out_weight, d_proj, block_section, section_parent, xref_owner, xref_block, xref_valid):
    key_value_width = KEY_VALUE_HEADS * HEAD_DIMENSION
    blk_width = BLK * key_value_width
    behind = LOOK - 1
    key_count = LOOK + ANC + XREF
    zero = jnp.zeros((), jnp.int32)
    section_ids = jnp.arange(SECTIONS, dtype=jnp.int32)
    member = (section_ids[:, None] == block_section[None, :]).astype(jnp.float32)
    counts = lax.optimization_barrier(jnp.sum(member, axis=1))
    root_counts = jnp.sqrt(counts)

    def summarize(array):
        flat = array.reshape(BLOCKS, blk_width).astype(jnp.float32)
        summed = jnp.dot(member, flat, precision=lax.Precision.HIGHEST) / root_counts[:, None]
        return summed.astype(jnp.bfloat16).reshape(SECTIONS, BLK, key_value_width)
    summary_keys = summarize(keys)
    summary_values = summarize(values)
    chain = [block_section]
    for depth_idx in range(1, ANC):
        prior = chain[-1]
        chain.append(jnp.where(prior >= 0, section_parent[jnp.clip(prior, 0)], -1))
    ancestors = jnp.stack(chain, axis=1)
    targets = xref_owner.reshape(BLOCKS, XREF) * BPD + xref_block
    key_blocks = keys.reshape(BLOCKS, BLK, key_value_width)
    value_blocks = values.reshape(BLOCKS, BLK, key_value_width)
    pad_keys = jnp.concatenate([jnp.zeros((behind, BLK, key_value_width), jnp.bfloat16), key_blocks])
    pad_values = jnp.concatenate([jnp.zeros((behind, BLK, key_value_width), jnp.bfloat16), value_blocks])
    padded_sec = jnp.concatenate([jnp.full((behind,), -1, jnp.int32), block_section])
    positions = jnp.arange(BLK)
    causal = positions[None, :] <= positions[:, None]
    is_last = jnp.arange(LOOK) == LOOK - 1

    def step(carry, block):
        grad_keys, grad_values, up_keys, up_values = carry
        own_keys = lax.dynamic_slice(pad_keys, (block, zero, zero), (LOOK, BLK, key_value_width))
        own_values = lax.dynamic_slice(pad_values, (block, zero, zero), (LOOK, BLK, key_value_width))
        own_sec = lax.dynamic_slice(padded_sec, (block,), (LOOK,))
        chosen_ups = ancestors[block]
        safe_ups = jnp.clip(chosen_ups, 0)
        refs = targets[block]
        key_set = jnp.concatenate([own_keys, summary_keys[safe_ups], key_blocks[refs]], axis=0)
        value_set = jnp.concatenate([own_values, summary_values[safe_ups], value_blocks[refs]], axis=0)
        own_ok = own_sec == block_section[block]
        own_allowed = own_ok[None, :, None] & (jnp.logical_not(is_last)[None, :, None] | causal[:, None, :])
        up_allowed = jnp.broadcast_to((chosen_ups >= 0)[None, :, None], (BLK, ANC, BLK))
        ref_allowed = jnp.broadcast_to((xref_valid[block] > 0)[None, :, None], (BLK, XREF, BLK))
        allowed = jnp.concatenate([own_allowed, up_allowed, ref_allowed], axis=1).reshape(BLK, key_count * BLK)
        query_block = lax.dynamic_slice(queries, (block * BLK, zero), (BLK, QUERY_HEAD_COUNT * HEAD_DIMENSION))
        attn = forward_block(query_block, key_set, value_set, allowed)
        projected = jnp.dot(attn, out_weight, preferred_element_type=jnp.float32).astype(jnp.bfloat16)
        cotangent = lax.dynamic_slice(d_proj, (block * BLK, zero), (BLK, OUTW))
        d_attn = jnp.dot(cotangent, out_weight.T, preferred_element_type=jnp.float32).astype(jnp.bfloat16)
        grad_query, key_terms, value_terms = backward_block(query_block, key_set, value_set, allowed, attn, d_attn)

        def absorb(grads, ups_acc, terms):
            terms = terms.reshape(key_count, BLK, key_value_width)
            window = lax.dynamic_slice(grads, (block, zero, zero), (LOOK, BLK, key_value_width))
            grads = lax.dynamic_update_slice(grads, window + terms[:LOOK], (block, zero, zero))
            ups_acc = ups_acc.at[safe_ups].add(terms[LOOK:LOOK + ANC])
            rounded = lax.optimization_barrier(terms[LOOK + ANC:].astype(jnp.bfloat16)).astype(jnp.float32)
            grads = grads.at[refs + behind].add(rounded)
            return (grads, ups_acc)
        grad_keys, up_keys = absorb(grad_keys, up_keys, key_terms)
        grad_values, up_values = absorb(grad_values, up_values, value_terms)
        return ((grad_keys, grad_values, up_keys, up_values), (projected, grad_query))
    start_grads = jnp.zeros((BLOCKS + behind, BLK, key_value_width), jnp.float32)
    start_ups = jnp.zeros((SECTIONS, BLK, key_value_width), jnp.float32)
    carry, outputs = lax.scan(step, (start_grads, start_grads, start_ups, start_ups), jnp.arange(BLOCKS, dtype=jnp.int32))
    grad_keys, grad_values, up_keys, up_values = carry
    projs, grad_queries = outputs
    spread_down = member.T / root_counts[None, :]

    def finish(grads, ups_acc):
        from_ups = jnp.dot(spread_down, ups_acc.reshape(SECTIONS, blk_width), precision=lax.Precision.HIGHEST)
        return (grads[behind:].reshape(BLOCKS, blk_width) + from_ups).astype(jnp.bfloat16).reshape(DOCUMENT_TOKENS, key_value_width)
    return (projs.reshape(DOCUMENT_TOKENS, OUTW), grad_queries.reshape(DOCUMENT_TOKENS, QUERY_HEAD_COUNT * HEAD_DIMENSION), finish(grad_keys, up_keys), finish(grad_values, up_values))
```

```python
import functools
import jax, jax.numpy as jnp
from jax import lax
from jax.experimental import pallas as pl
from jax.experimental.pallas import tpu as pltpu
from jax.sharding import PartitionSpec as P
F32, BF = jnp.float32, jnp.bfloat16
MESH = pl.DeviceIdType.MESH
RING = 4


HD = 128
BLK = 128
LOG2E = 1.4426950408889634


def attention_kernel(NBLK, NSEC, NQ, G, XR, meta, q_ref, k_hbm, v_hbm, do_ref, attn_ref, dq_ref, dk_ref, dv_ref,
                     kc, vc, ak, av, sbuf, qs, dos, dot_t, ot, mrun, lrun, slots, counts, first, length, sems):
    scaling = HD ** -0.5
    NT = (((1,), (1,)), ((), ()))
    TN = (((0,), (0,)), ((), ()))
    NN = (((1,), (0,)), ((), ()))

    def mm(a, b, dims):
        return lax.dot_general(a, b, dims, preferred_element_type=F32)

    load_k = pltpu.make_async_copy(k_hbm, kc.at[pl.ds(0, NBLK * BLK)], sems.at[0])
    load_v = pltpu.make_async_copy(v_hbm, vc.at[pl.ds(0, NBLK * BLK)], sems.at[1])
    load_k.start()
    load_v.start()

    @pl.loop(0, NSEC)
    def _(s):
        length[s] = 0
        first[s] = 0

    @pl.loop(0, NBLK)
    def _(c):
        s = meta[4, c]
        n = length[s]

        @pl.when(n == 0)
        def _():
            first[s] = c
        length[s] = n + 1

    @pl.loop(0, NQ)
    def _(b):
        g = meta[6, 0] + b
        mine = meta[4, g]
        slots[b, 0] = g
        slots[b, 1] = NBLK + mine
        n = jnp.int32(2)
        for w in (1, 2, 3):
            c = g - w
            cs = jnp.maximum(c, 0)
            slots[b, n] = cs
            n = n + jnp.where((c >= 0) & (meta[4, cs] == mine), 1, 0)
        up = meta[5, mine]
        slots[b, n] = NBLK + jnp.maximum(up, 0)
        n = n + jnp.where(up >= 0, 1, 0)
        row = lax.div(b, 4) * 8 + lax.rem(b, 4)
        for j in range(XR):
            t = meta[row, j]
            slots[b, n] = jnp.maximum(t, 0) + 256
            n = n + jnp.where(t >= 0, 1, 0)
        counts[b] = n

    @pl.loop(0, (NBLK + NSEC) // 4)
    def _(i):
        at = pl.ds(pl.multiple_of(i * 512, 512), 512)
        ak[at, :] = jnp.zeros((512, HD), F32)
        av[at, :] = jnp.zeros((512, HD), F32)

    load_k.wait()
    load_v.wait()

    def block(ref, i):
        return ref[pl.ds(pl.multiple_of(i * BLK, BLK), BLK), :]

    def root(s):
        return jnp.sqrt(jnp.full((8, HD), jnp.maximum(length[s], 1)).astype(F32))[:1]

    @pl.loop(0, NSEC)
    def _(s):
        for ref in (kc, vc):
            total = lax.fori_loop(first[s], first[s] + length[s],
                                  lambda c, t: t + block(ref, c).astype(F32), jnp.zeros((BLK, HD), F32))
            ref[pl.ds(pl.multiple_of((NBLK + s) * BLK, BLK), BLK), :] = (total / root(s)).astype(BF)

    W = G * BLK
    row_id = lax.broadcasted_iota(jnp.int32, (2 * BLK, BLK), 0)
    col_id = lax.broadcasted_iota(jnp.int32, (2 * BLK, BLK), 1)
    open_one = (row_id <= col_id) | (row_id >= BLK)
    open_all = jnp.concatenate([open_one] * G, axis=1)
    c2 = scaling * LOG2E

    def fold(op, s):
        return op(s.reshape(s.shape[0] // 8, 8, W), axis=0)

    @pl.loop(0, NQ)
    def _(b):
        base = pl.multiple_of(b * BLK, BLK)
        for g in range(G):
            part = slice(g * BLK, (g + 1) * BLK)
            qs[part, :] = q_ref[pl.ds(base, BLK), part]
            d = do_ref[pl.ds(base, BLK), part]
            dos[part, :] = d
            dot_t[:, part] = d.astype(F32).T.astype(BF)
        n = counts[b]
        pairs = lax.div(n, 2)
        odd = lax.rem(n, 2) == 1

        def idx(i):
            return slots[b, i] & 255

        def pair(ref, j):
            return jnp.concatenate([block(ref, idx(2 * j)), block(ref, idx(2 * j + 1))], axis=0)

        def at2(j):
            return pl.ds(pl.multiple_of(j * 2 * BLK, 2 * BLK), 2 * BLK)

        last = pl.ds(pl.multiple_of((n - 1) * BLK, BLK), BLK)

        s0 = jnp.where(open_all, mm(pair(kc, 0), qs[...], NT), -1e30)
        sbuf[at2(0), :] = s0

        def score(j, m):
            s = mm(pair(kc, j), qs[...], NT)
            sbuf[at2(j), :] = s
            return jnp.maximum(m, fold(jnp.max, s))
        mrun[...] = lax.fori_loop(1, pairs, score, fold(jnp.max, s0))

        @pl.when(odd)
        def _():
            s = mm(block(kc, idx(n - 1)), qs[...], NT)
            sbuf[last, :] = s
            mrun[...] = jnp.maximum(mrun[...], fold(jnp.max, s))
        top = jnp.max(mrun[...], axis=0, keepdims=True) * c2

        def weigh(rows, v):
            e = jnp.exp2(sbuf[rows, :] * c2 - top)
            sbuf[rows, :] = e
            return fold(jnp.sum, e), mm(v, e.astype(BF), TN)

        lrun[...], ot[...] = weigh(at2(0), pair(vc, 0))

        def forward(j, l):
            dl, o = weigh(at2(j), pair(vc, j))
            ot[...] += o
            return l + dl
        lrun[...] = lax.fori_loop(1, pairs, forward, lrun[...])

        @pl.when(odd)
        def _():
            dl, o = weigh(last, block(vc, idx(n - 1)))
            ot[...] += o
            lrun[...] += dl
        rl = 1.0 / jnp.sum(lrun[...], axis=0, keepdims=True)
        o_t = (ot[...] * rl).astype(BF).astype(F32)
        delta = jnp.sum(o_t * dot_t[...].astype(F32), axis=0, keepdims=True) * scaling
        for g in range(G):
            part = slice(g * BLK, (g + 1) * BLK)
            attn_ref[pl.ds(base, BLK), part] = o_t[:, part].T.astype(BF)

        def put(acc, i, term):
            slot = slots[b, i]
            where = pl.ds(pl.multiple_of((slot & 255) * BLK, BLK), BLK)
            term = jnp.where(slot >= 256, term.astype(BF).astype(F32), term)
            acc[where, :] += term

        def back(rows, k, v):
            p = sbuf[rows, :] * rl
            dp = mm(v, dot_t[...], NN)
            ds = (p * (dp * scaling - delta)).astype(BF)
            return mm(ds, qs[...], NN), mm(p.astype(BF), dos[...], NN), mm(k, ds, TN)

        ot[...] = jnp.zeros((HD, W), F32)

        def backward(j, carry):
            dk, dv, dq = back(at2(j), pair(kc, j), pair(vc, j))
            for h in range(2):
                put(ak, 2 * j + h, dk[h * BLK:(h + 1) * BLK])
                put(av, 2 * j + h, dv[h * BLK:(h + 1) * BLK])
            ot[...] += dq
            return carry
        lax.fori_loop(0, pairs, backward, 0)

        @pl.when(odd)
        def _():
            dk, dv, dq = back(last, block(kc, idx(n - 1)), block(vc, idx(n - 1)))
            put(ak, n - 1, dk)
            put(av, n - 1, dv)
            ot[...] += dq
        for g in range(G):
            part = slice(g * BLK, (g + 1) * BLK)
            dq_ref[pl.ds(base, BLK), part] = ot[:, part].T.astype(BF)

    @pl.loop(0, NBLK)
    def _(c):
        s = meta[4, c]
        share = 1.0 / root(s)
        at = pl.ds(pl.multiple_of(c * BLK, BLK), BLK)
        dk_ref[at, :] = (ak[at, :] + block(ak, NBLK + s) * share).astype(BF)
        dv_ref[at, :] = (av[at, :] + block(av, NBLK + s) * share).astype(BF)


def attention(meta, q, k, v, do, NSEC=16, XR=12):
    NBLK = k.shape[0] // BLK
    NQ = q.shape[0] // BLK
    G = q.shape[1] // HD
    W = G * BLK
    slots_most = 6 + XR
    vm = pl.BlockSpec(memory_space=pltpu.VMEM)
    return pl.pallas_call(
        functools.partial(attention_kernel, NBLK, NSEC, NQ, G, XR),
        out_shape=(jax.ShapeDtypeStruct(q.shape, BF), jax.ShapeDtypeStruct(q.shape, BF),
                   jax.ShapeDtypeStruct(k.shape, BF), jax.ShapeDtypeStruct(k.shape, BF)),
        in_specs=[pl.BlockSpec(memory_space=pltpu.SMEM), vm, pl.BlockSpec(memory_space=pl.ANY),
                  pl.BlockSpec(memory_space=pl.ANY), vm],
        out_specs=(vm, vm, vm, vm),
        scratch_shapes=[
            pltpu.VMEM(((NBLK + NSEC) * BLK, HD), BF),
            pltpu.VMEM(((NBLK + NSEC) * BLK, HD), BF),
            pltpu.VMEM(((NBLK + NSEC) * BLK, HD), F32),
            pltpu.VMEM(((NBLK + NSEC) * BLK, HD), F32),
            pltpu.VMEM((slots_most * BLK, W), F32),
            pltpu.VMEM((W, HD), BF),
            pltpu.VMEM((W, HD), BF),
            pltpu.VMEM((HD, W), BF),
            pltpu.VMEM((HD, W), F32),
            pltpu.VMEM((8, W), F32),
            pltpu.VMEM((8, W), F32),
            pltpu.SMEM((NQ, 24), jnp.int32),
            pltpu.SMEM((NQ,), jnp.int32),
            pltpu.SMEM((NSEC,), jnp.int32),
            pltpu.SMEM((NSEC,), jnp.int32),
            pltpu.SemaphoreType.DMA((2,)),
        ],
        compiler_params=pltpu.CompilerParams(vmem_limit_bytes=60 * 1024 * 1024),
        cost_estimate=pl.CostEstimate(flops=18_000_000_000, bytes_accessed=24_000_000, transcendentals=12_000_000),
    )(meta, q, k, v, do)


class Links:
    def __init__(self, send_sems, recv_sems):
        s = lax.axis_index("seq")
        self.y = lax.axis_index("head")
        self.x = s // 8
        self.z = (s // 2) % RING
        self.c = s % 2
        self.send_sems, self.recv_sems = send_sems, recv_sems
        self.used = 0
        self.sent = []

    def device(self, axis, step):
        x, z, y, c = self.x, self.z, self.y, self.c
        if axis == "x":
            x = (x + step) % RING
        elif axis == "z":
            z = (z + step) % RING
        elif axis == "y":
            y = (y + step) % RING
        else:
            c = 1 - c
        return ((x * RING + z) * 2 + c, y)

    def everyone(self):
        return [self.device(a, d) for a in "xzy" for d in (1, RING - 1)] + [self.device("c", 1)]

    def barrier(self):
        sem = pltpu.get_barrier_semaphore()
        for device in self.everyone():
            pl.semaphore_signal(sem, inc=1, device_id=device, device_id_type=MESH)
        pl.semaphore_wait(sem, 7)

    def number(self):
        self.used += 1
        return self.used - 1

    def send(self, number, src, dst, axis, step):
        copy = pltpu.make_async_remote_copy(
            src_ref=src, dst_ref=dst, send_sem=self.send_sems.at[number], recv_sem=self.recv_sems.at[number],
            device_id=self.device(axis, step), device_id_type=MESH)
        copy.start()
        self.sent.append(copy)

    def arrived(self, number, dst):
        pltpu.make_async_remote_copy(
            src_ref=dst, dst_ref=dst, send_sem=self.send_sems.at[number], recv_sem=self.recv_sems.at[number],
            device_id=self.device("c", 1), device_id_type=MESH).wait_recv()

    def finish(self):
        for copy in self.sent:
            copy.wait_send()


class Gather:
    def __init__(self, links, array, rows, pitch, offset, split, a, b):
        self.L, self.array, self.rows, self.pitch, self.offset, self.split = links, array, rows, pitch, offset, split
        self.a, self.b = a, b
        self.na = [links.number() for _ in range(4)]
        self.nb = [[links.number() for _ in range(4)] for _ in range(4)]

    def at(self, da, db, half=None):
        L = self.L
        move = {self.a: da, self.b: db}
        x, z = (L.x + move["x"]) % RING, (L.z + move["z"]) % RING
        start, count = self.offset, self.rows
        if half == 0:
            count = self.split
        elif half == 1:
            start, count = self.offset + self.split, self.rows - self.split
        return self.array.at[pl.ds(pl.multiple_of((x * RING + z) * self.pitch + start, 16), count), :]

    def put(self, number, axis, step, da, db, half=None):
        self.L.send(number, self.at(da, db, half), self.at(da, db, half), axis, step)

    def begin(self):
        self.put(self.na[0], self.a, 1, 0, 0)
        self.put(self.na[1], self.a, 3, 0, 0)

    def spread(self, i, da):
        self.put(self.nb[i][0], self.b, 1, da, 0)
        self.put(self.nb[i][1], self.b, 3, da, 0)

    def near(self):
        self.L.arrived(self.na[0], self.at(3, 0))
        self.put(self.na[2], self.a, 1, 3, 0, 0)
        self.L.arrived(self.na[1], self.at(1, 0))
        self.put(self.na[3], self.a, 3, 1, 0, 1)
        self.spread(0, 0)
        self.spread(1, 3)
        self.spread(2, 1)

    def far(self):
        self.L.arrived(self.na[2], self.at(2, 0, 0))
        self.L.arrived(self.na[3], self.at(2, 0, 1))
        self.spread(3, 2)

    def relay(self, i):
        da = (0, 3, 1, 2)[i]
        self.L.arrived(self.nb[i][0], self.at(da, 3))
        self.put(self.nb[i][2], self.b, 1, da, 3, 0)
        self.L.arrived(self.nb[i][1], self.at(da, 1))
        self.put(self.nb[i][3], self.b, 3, da, 1, 1)

    def end(self, i):
        da = (0, 3, 1, 2)[i]
        self.L.arrived(self.nb[i][2], self.at(da, 2, 0))
        self.L.arrived(self.nb[i][3], self.at(da, 2, 1))


def gather_kernel(q, k, v, wt, dp, meta, qh, kall, vall, wall, dattn, metas, wbuf, dbuf, abuf, send_sems, recv_sems, own_sems):
    L = Links(send_sems, recv_sems)
    chip = L.x * RING + L.z
    other = 1 - L.c
    T = k.shape[0]
    HD = kall.shape[1]
    W = qh.shape[1]
    C = wt.shape[0]
    D = dp.shape[1]
    L.barrier()

    pairs = []

    def split(src, width, dst, first, rows):
        at = dst.at[pl.ds(pl.multiple_of(first, 16), rows), :]
        pairs.append((L.number(), src, width, dst, at, rows))

    mine = chip * 2 * T + L.c * T
    split(wt, W, wbuf, chip * 2 * C + L.c * C, C)
    split(k, HD, kall, mine, T)
    split(v, HD, vall, mine, T)
    split(q, W, qh, L.c * T, T)
    own = []
    for i, (number, src, width, dst, at, rows) in enumerate(pairs):
        L.send(number, src.at[:, pl.ds(pl.multiple_of(other * width, 128), width)], at, "c", 1)
        copy = pltpu.make_async_copy(src.at[:, pl.ds(pl.multiple_of(L.c * width, 128), width)], at, own_sems.at[i])
        copy.start()
        own.append(copy)
    n_meta = L.number()
    mrow = metas.at[L.c]
    L.send(n_meta, meta, mrow, "c", 1)
    own_meta = pltpu.make_async_copy(meta, mrow, own_sems.at[4])
    own_meta.start()

    def piece(core, dy, half=None):
        ref = dbuf.at[core * RING + (L.y + dy) % RING]
        if half is None:
            return ref
        return ref.at[pl.ds(half * (T // 2), T // 2), :]

    ny = [L.number() for _ in range(4)]
    nc = [L.number() for _ in range(4)]
    L.send(ny[0], dp, piece(L.c, 0), "y", 1)
    L.send(ny[1], dp, piece(L.c, 0), "y", 3)
    L.send(nc[0], dp, piece(L.c, 0), "c", 1)
    own_d = pltpu.make_async_copy(dp, piece(L.c, 0), own_sems.at[5])
    own_d.start()

    sibling = [chip * 2 * C + other * C, chip * 2 * T + other * T, chip * 2 * T + other * T, other * T]

    def both(i):
        number, src, width, dst, at, rows = pairs[i]
        L.arrived(number, dst.at[pl.ds(pl.multiple_of(sibling[i], 16), rows), :])
        own[i].wait()

    first_w = (C // 2 + 15) // 16 * 16
    w0 = Gather(L, wbuf, C, 2 * C, 0, first_w, "x", "z")
    w1 = Gather(L, wbuf, C, 2 * C, C, first_w, "z", "x")
    gk = Gather(L, kall, 2 * T, 2 * T, 0, T, "x", "z")
    gv = Gather(L, vall, 2 * T, 2 * T, 0, T, "z", "x")
    both(0)
    w0.begin()
    w1.begin()
    both(1)
    gk.begin()
    both(2)
    gv.begin()
    w0.near()
    w1.near()
    w0.far()
    w1.far()
    L.arrived(ny[0], piece(L.c, 3))
    L.send(ny[2], piece(L.c, 3, 0), piece(L.c, 3, 0), "y", 1)
    L.arrived(ny[1], piece(L.c, 1))
    L.send(ny[3], piece(L.c, 1, 1), piece(L.c, 1, 1), "y", 3)
    L.send(nc[1], piece(L.c, 3), piece(L.c, 3), "c", 1)
    L.send(nc[2], piece(L.c, 1), piece(L.c, 1), "c", 1)
    gk.near()
    gv.near()
    for i in range(4):
        w0.relay(i)
        w1.relay(i)
    gk.far()
    gv.far()
    L.arrived(ny[2], piece(L.c, 2, 0))
    L.arrived(ny[3], piece(L.c, 2, 1))
    L.send(nc[3], piece(L.c, 2), piece(L.c, 2), "c", 1)
    for i in range(2):
        gk.relay(i)
        gv.relay(i)
    for i in range(4):
        w0.end(i)
        w1.end(i)
    own_d.wait()
    for i, dy in enumerate((0, 3, 1, 2)):
        L.arrived(nc[i], piece(other, dy))
    keep = pltpu.make_async_copy(wbuf, wall, own_sems.at[6])
    keep.start()

    step = 256

    def product(core, t):
        rows = pl.ds(pl.multiple_of(t * step, step), step)
        total = jnp.zeros((step, W), F32)
        for y in range(RING):
            total += jnp.dot(dbuf[core * RING + y, rows, :], wbuf[y * D:(y + 1) * D, :], preferred_element_type=F32)
        abuf[pl.ds(pl.multiple_of(core * T + t * step, step), step), :] = total.astype(BF)

    def products(core):
        @pl.loop(0, T // step)
        def _(t):
            product(core, t)

    products(0)
    for i in range(2, 4):
        gk.relay(i)
        gv.relay(i)
    products(1)
    save = pltpu.make_async_copy(abuf, dattn, own_sems.at[7])
    save.start()
    for i in range(4):
        gk.end(i)
        gv.end(i)
    both(3)
    L.arrived(n_meta, metas.at[other])
    own_meta.wait()
    keep.wait()
    save.wait()
    L.finish()


def gather(q, k, v, wt, dp, meta, seq):
    T = k.shape[0]
    HD = k.shape[1] // 2
    W = q.shape[1] // 2
    C = wt.shape[0]
    D = dp.shape[1]
    anywhere = pl.BlockSpec(memory_space=pl.ANY)
    sems = 128
    return pl.pallas_call(
        gather_kernel,
        out_shape=(
            jax.ShapeDtypeStruct((2 * T, W), BF),
            jax.ShapeDtypeStruct((seq * T, HD), BF),
            jax.ShapeDtypeStruct((seq * T, HD), BF),
            jax.ShapeDtypeStruct((seq * C, W), BF),
            jax.ShapeDtypeStruct((2 * T, W), BF),
            jax.ShapeDtypeStruct((2,) + meta.shape, jnp.int32),
        ),
        in_specs=[anywhere] * 6,
        out_specs=(anywhere,) * 6,
        scratch_shapes=[
            pltpu.VMEM((seq * C, W), BF),
            pltpu.VMEM((2 * RING, T, D), BF),
            pltpu.VMEM((2 * T, W), BF),
            pltpu.SemaphoreType.DMA((sems,)),
            pltpu.SemaphoreType.DMA((sems,)),
            pltpu.SemaphoreType.DMA((8,)),
        ],
        compiler_params=pltpu.CompilerParams(
            collective_id=0, has_side_effects=True, vmem_limit_bytes=40 * 1024 * 1024),
        cost_estimate=pl.CostEstimate(flops=3_400_000_000, bytes_accessed=40_000_000, transcendentals=0),
    )(q, k, v, wt, dp, meta)


class Scatter:
    def __init__(self, links, source, buf, far, near, far2, near2, final, a, b, load_sem):
        self.L, self.source, self.buf = links, source, buf
        self.farr, self.nearr, self.far2, self.near2, self.final = far, near, far2, near2, final
        self.a, self.b = a, b
        self.rows = final.shape[0]
        self.nb = [[links.number() for _ in range(4)] for _ in range(4)]
        self.na = [links.number() for _ in range(4)]
        self.load = pltpu.make_async_copy(source, buf, load_sem)
        self.load.start()

    def where(self, da, db, half=None):
        L = self.L
        move = {self.a: da, self.b: db}
        x, z = (L.x + move["x"]) % RING, (L.z + move["z"]) % RING
        start, count = 0, self.rows
        if half is not None:
            count = self.rows // 2
            start = half * count
        return pl.ds(pl.multiple_of((x * RING + z) * self.rows + start, 16), count)

    def half(self, h):
        return pl.ds(h * (self.rows // 2), self.rows // 2)

    def begin(self, i):
        da = (2, 3, 1, 0)[i]
        for h, step in ((0, 1), (1, 3)):
            self.L.send(self.nb[i][h], self.source.at[self.where(da, 2, h), :], self.farr.at[i, h], self.b, step)

    def loaded(self):
        self.load.wait()

    def pass_on(self, i):
        da = (2, 3, 1, 0)[i]
        for h, step in ((0, 1), (1, 3)):
            self.L.arrived(self.nb[i][h], self.farr.at[i, h])
            at = self.where(da, step, h)
            self.buf[at, :] = (self.buf[at, :].astype(F32) + self.farr[i, h].astype(F32)).astype(BF)
            self.L.send(self.nb[i][2 + h], self.buf.at[self.where(da, step), :], self.nearr.at[i, h], self.b, step)

    def total(self, i, da, h):
        at = self.where(da, 0, h)
        part = self.half(h)
        return (self.buf[at, :].astype(F32) + self.nearr[i, 0, part, :].astype(F32)
                + self.nearr[i, 1, part, :].astype(F32))

    def close(self, i):
        da = (2, 3, 1, 0)[i]
        for h in range(2):
            self.L.arrived(self.nb[i][2 + h], self.nearr.at[i, h])
        if i == 0:
            for h, step in ((0, 1), (1, 3)):
                at = self.where(da, 0, h)
                self.buf[at, :] = self.total(i, da, h).astype(BF)
                self.L.send(self.na[h], self.buf.at[at, :], self.far2.at[h], self.a, step)
        elif i < 3:
            take = 1 if da == 3 else 0
            self.L.arrived(self.na[take], self.far2.at[take])
            for h in range(2):
                value = self.total(i, da, h)
                if h == take:
                    value += self.far2[take].astype(F32)
                self.buf[self.where(da, 0, h), :] = value.astype(BF)
            self.L.send(self.na[2 + take], self.buf.at[self.where(da, 0), :], self.near2.at[take], self.a, da)

    def finish(self):
        for take in range(2):
            self.L.arrived(self.na[2 + take], self.near2.at[take])
        for h in range(2):
            part = self.half(h)
            self.final[part, :] = (self.total(3, 0, h) + self.near2[0, part, :].astype(F32)
                                   + self.near2[1, part, :].astype(F32)).astype(BF)


def scatter_kernel(dk, dv, attn, wall, dq, proj, dqo, dko, dvo,
                   bufk, bufv, farr, nearr, far2, near2, final, there, here, halves, wholes, result,
                   send_sems, recv_sems, own_sems):
    L = Links(send_sems, recv_sems)
    other = 1 - L.c
    T = proj.shape[0]
    D = proj.shape[1]
    W = dq.shape[1]
    HD = dk.shape[1]
    L.barrier()
    sk = Scatter(L, dk, bufk, farr.at[0], nearr.at[0], far2.at[0], near2.at[0], final.at[0], "x", "z", own_sems.at[0])
    sv = Scatter(L, dv, bufv, farr.at[1], nearr.at[1], far2.at[1], near2.at[1], final.at[1], "z", "x", own_sems.at[1])
    for i in range(4):
        sk.begin(i)
        sv.begin(i)

    def rows_of(core):
        return pl.ds(pl.multiple_of(core * T, 16), T)

    def heads(ref, core, width):
        return ref.at[:, pl.ds(pl.multiple_of(core * width, 128), width)]

    n_q = L.number()
    L.send(n_q, dq.at[rows_of(other), :], heads(dqo, L.c, W), "c", 1)
    own_q = pltpu.make_async_copy(dq.at[rows_of(L.c), :], heads(dqo, L.c, W), own_sems.at[2])
    own_q.start()

    n_there = [L.number() for _ in range(4)]
    ny = [L.number() for _ in range(4)]
    order = (2, 1, 3, 0)

    def product(core, dy):
        y = (L.y + dy) % RING
        w = wall[pl.ds(pl.multiple_of(y * D, 16), D), :]
        return lax.dot_general(attn[rows_of(core), :], w, (((1,), (1,)), ((), ())), preferred_element_type=F32)

    def away(i):
        here[i] = product(other, order[i]).astype(BF)
        L.send(n_there[i], here.at[i], there.at[i], "c", 1)

    def mine(i):
        value = product(L.c, order[i])
        L.arrived(n_there[i], there.at[i])
        return value + there[i].astype(F32)

    mid = T // 2
    away(0)
    sk.loaded()
    sv.loaded()
    sk.pass_on(0)
    sv.pass_on(0)
    away(1)
    sk.pass_on(1)
    sv.pass_on(1)
    away(2)
    away(3)
    sk.pass_on(2)
    sv.pass_on(2)
    result[0] = mine(0).astype(BF)
    L.send(ny[0], result.at[0, pl.ds(0, mid), :], halves.at[0], "y", 1)
    L.send(ny[1], result.at[0, pl.ds(mid, mid), :], halves.at[1], "y", 3)
    sk.pass_on(3)
    sv.pass_on(3)
    sk.close(0)
    sv.close(0)
    value = mine(1)
    L.arrived(ny[0], halves.at[0])
    result[1] = jnp.concatenate([value[:mid] + halves[0].astype(F32), value[mid:]], axis=0).astype(BF)
    L.send(ny[2], result.at[1], wholes.at[0], "y", 1)
    value = mine(2)
    L.arrived(ny[1], halves.at[1])
    result[2] = jnp.concatenate([value[:mid], value[mid:] + halves[1].astype(F32)], axis=0).astype(BF)
    L.send(ny[3], result.at[2], wholes.at[1], "y", 3)
    for i in (1, 2):
        sk.close(i)
        sv.close(i)
    value = mine(3)
    L.arrived(ny[2], wholes.at[0])
    L.arrived(ny[3], wholes.at[1])
    result[3] = (value + wholes[0].astype(F32) + wholes[1].astype(F32)).astype(BF)
    own_p = pltpu.make_async_copy(result.at[3], proj, own_sems.at[3])
    own_p.start()
    outs = []
    for j, (s, out) in enumerate(((sk, dko), (sv, dvo))):
        s.close(3)
        s.finish()
        n = L.number()
        L.send(n, final.at[j, rows_of(other), :], heads(out, L.c, HD), "c", 1)
        own = pltpu.make_async_copy(final.at[j, rows_of(L.c), :], heads(out, L.c, HD), own_sems.at[4 + j])
        own.start()
        outs.append((n, out, own))
    L.arrived(n_q, heads(dqo, other, W))
    own_q.wait()
    own_p.wait()
    for n, out, own in outs:
        L.arrived(n, heads(out, other, HD))
        own.wait()
    L.finish()


def scatter(dk, dv, attn, wall, dq, D):
    T = dq.shape[0] // 2
    W = dq.shape[1]
    HD = dk.shape[1]
    anywhere = pl.BlockSpec(memory_space=pl.ANY)
    vmem = pl.BlockSpec(memory_space=pltpu.VMEM)
    sems = 64
    return pl.pallas_call(
        scatter_kernel,
        out_shape=(
            jax.ShapeDtypeStruct((T, D), BF),
            jax.ShapeDtypeStruct((T, 2 * W), BF),
            jax.ShapeDtypeStruct((T, 2 * HD), BF),
            jax.ShapeDtypeStruct((T, 2 * HD), BF),
        ),
        in_specs=[anywhere, anywhere, vmem, vmem, anywhere],
        out_specs=(anywhere,) * 4,
        scratch_shapes=[
            pltpu.VMEM(dk.shape, BF),
            pltpu.VMEM(dk.shape, BF),
            pltpu.VMEM((2, 4, 2, T, HD), BF),
            pltpu.VMEM((2, 4, 2, 2 * T, HD), BF),
            pltpu.VMEM((2, 2, T, HD), BF),
            pltpu.VMEM((2, 2, 2 * T, HD), BF),
            pltpu.VMEM((2, 2 * T, HD), BF),
            pltpu.VMEM((4, T, D), BF),
            pltpu.VMEM((4, T, D), BF),
            pltpu.VMEM((2, T // 2, D), BF),
            pltpu.VMEM((2, T, D), BF),
            pltpu.VMEM((4, T, D), BF),
            pltpu.SemaphoreType.DMA((sems,)),
            pltpu.SemaphoreType.DMA((sems,)),
            pltpu.SemaphoreType.DMA((6,)),
        ],
        compiler_params=pltpu.CompilerParams(
            collective_id=1, has_side_effects=True, vmem_limit_bytes=56 * 1024 * 1024),
        cost_estimate=pl.CostEstimate(flops=3_400_000_000, bytes_accessed=40_000_000, transcendentals=0),
    )(dk, dv, attn, wall, dq)


def on_device(queries, keys, values, out_weight, d_proj, block_section, section_parent, xref_owner, xref_block, xref_valid):
    seq = lax.axis_size("seq")
    blocks, xrefs = xref_block.shape
    target = jnp.where(xref_valid > 0, xref_owner.reshape(blocks, xrefs) * blocks + xref_block, -1)
    first = (lax.axis_index("seq") // 2) * 2 * blocks
    meta = jnp.concatenate([
        jnp.pad(target, ((0, 0), (0, 128 - xrefs))),
        block_section[None, :],
        jnp.pad(section_parent, (0, 128 - section_parent.shape[0]))[None, :],
        jnp.full((2, 128), first, jnp.int32),
    ], axis=0)
    qh, kall, vall, wall, d_attn, metas = gather(queries, keys, values, out_weight.T, d_proj, meta, seq)
    attn, dq, dk, dv = attention(metas.reshape(16, 128), qh, kall, vall, d_attn)
    return scatter(dk, dv, attn, wall, dq, d_proj.shape[1])


def solution(mesh):
    split = P("seq", "head")
    rows = P("seq", None)
    return jax.shard_map(
        on_device, mesh=mesh,
        in_specs=(split, split, split, P("head", "seq"), split, P(), P(), rows, rows, rows),
        out_specs=(split,) * 4, check_vma=False)
```

```python
import functools
import jax, jax.numpy as jnp
from jax import lax
from jax.experimental import pallas as pl
from jax.experimental.pallas import tpu as pltpu
from jax.sharding import PartitionSpec as P
F32, BF = jnp.float32, jnp.bfloat16
MESH = pl.DeviceIdType.MESH
RING = 4


HD = 128
BLK = 128
CHUNK = 4
BOTH = 2


def attention_kernel(NBLK, NSEC, NQ, G, XR, meta, q_hbm, k_hbm, v_hbm, do_hbm, attn_hbm, dq_hbm, dk_hbm, dv_hbm,
                     kc, vc, ak, av, sbuf0, sbuf1, q_ref, do_ref, attn_ref, dq_ref, dk_ref, dv_ref,
                     qs_t, dot_t, ot0, ot1, shares, slots, counts, first, stop, done, sems):
    scaling = HD ** -0.5
    sbuf, ot = (sbuf0, sbuf1), (ot0, ot1)
    NT = (((1,), (1,)), ((), ()))
    TN = (((0,), (0,)), ((), ()))
    NN = (((1,), (0,)), ((), ()))
    R = CHUNK * BLK

    def mm(a, b, dims):
        return lax.dot_general(a, b, dims, preferred_element_type=F32)

    loads = [pltpu.make_async_copy(src, dst, sems.at[i]) for i, (src, dst) in enumerate((
        (k_hbm, kc.at[pl.ds(0, NBLK * BLK)]), (v_hbm, vc.at[pl.ds(0, NBLK * BLK)]), (q_hbm, q_ref), (do_hbm, do_ref)))]
    for copy in loads:
        copy.start()

    @pl.loop(0, NSEC)
    def _(s):
        stop[s] = 0
        first[s] = 0
        done[s] = 0

    @pl.loop(0, NBLK // 8)
    def _(i):
        for h in range(8):
            c = i * 8 + h
            stop[meta[4, c]] = c + 1
            d = NBLK - 1 - c
            first[meta[4, d]] = d

    @pl.loop(0, NQ)
    def _(b):
        g = meta[6, 0] + b
        mine = meta[4, g]
        for j in range(32):
            slots[b, j] = g
        slots[b, 1] = NBLK + mine
        n = jnp.int32(2)
        for w in (1, 2, 3):
            c = g - w
            cs = jnp.maximum(c, 0)
            slots[b, n] = cs
            n = n + jnp.where((c >= 0) & (meta[4, cs] == mine), 1, 0)
        up = meta[5, mine]
        slots[b, n] = NBLK + jnp.maximum(up, 0)
        n = n + jnp.where(up >= 0, 1, 0)
        row = lax.div(b, 4) * 8 + lax.rem(b, 4)
        for j in range(XR):
            t = meta[row, j]
            slots[b, n] = jnp.maximum(t, 0) + 256
            n = n + jnp.where(t >= 0, 1, 0)
        slots[b, n] = g
        counts[b] = n

    @pl.loop(0, (NBLK + NSEC) // 4)
    def _(i):
        at = pl.ds(pl.multiple_of(i * 512, 512), 512)
        ak[at, :] = jnp.zeros((512, HD), F32)
        av[at, :] = jnp.zeros((512, HD), F32)

    for copy in loads:
        copy.wait()

    def span(i):
        return pl.ds(pl.multiple_of(i * BLK, BLK), BLK)

    def summarize(s):
        def add(c, t):
            return t[0] + kc[span(c), :].astype(F32), t[1] + vc[span(c), :].astype(F32)
        zero = jnp.zeros((BLK, HD), F32)
        tk, tv = lax.fori_loop(first[s], stop[s], add, (zero, zero))
        share = 1.0 / jnp.sqrt(jnp.full((8, HD), jnp.maximum(stop[s] - first[s], 1)).astype(F32))
        shares[s] = share
        kc[span(NBLK + s), :] = (tk * share[:1]).astype(BF)
        vc[span(NBLK + s), :] = (tv * share[:1]).astype(BF)
        done[s] = 1

    @pl.loop(0, 2 * NQ)
    def _(i):
        mine = meta[4, meta[6, 0] + lax.div(i, 2)]
        s = jnp.where(lax.rem(i, 2) == 0, mine, jnp.maximum(meta[5, mine], 0))

        @pl.when(done[s] == 0)
        def _():
            summarize(s)

    W = G * BLK
    row_id = lax.broadcasted_iota(jnp.int32, (BLK, BLK), 0)
    col_id = lax.broadcasted_iota(jnp.int32, (BLK, BLK), 1)
    causal = jnp.concatenate([row_id <= col_id] * G, axis=1)

    def fold(op, s):
        return op(s.reshape(s.shape[0] // 8, 8, W), axis=0)

    ones = jnp.ones((R, 16), BF)

    TWO = range(BOTH)

    @pl.loop(0, NQ // BOTH)
    def _(u):
        bs = [u * BOTH + t for t in TWO]
        bases = [pl.multiple_of(b * BLK, BLK) for b in bs]
        for t in TWO:
            for g in range(G):
                part = slice(g * BLK, (g + 1) * BLK)
                qs_t[t, :, part] = q_ref[pl.ds(bases[t], BLK), part].astype(F32).T.astype(BF)
                dot_t[t, :, part] = do_ref[pl.ds(bases[t], BLK), part].astype(F32).T.astype(BF)
        ns = [counts[b] for b in bs]
        most = ns[0]
        for n in ns[1:]:
            most = jnp.maximum(most, n)
        chunks = lax.div(most + CHUNK - 1, CHUNK)

        def chunk(t, ref, j):
            return jnp.concatenate([ref[span(slots[bs[t], CHUNK * j + h] & 255), :] for h in range(CHUNK)], axis=0)

        def rows(j):
            return pl.ds(pl.multiple_of(j * R, R), R)

        def scores(t, j):
            s = mm(chunk(t, kc, j), qs_t[t], NN) * scaling
            return jnp.concatenate([
                s[h * BLK:(h + 1) * BLK] + jnp.where(CHUNK * j + h < ns[t], 0.0, -1e30) for h in range(CHUNK)], axis=0)

        tops = []
        for t in TWO:
            s0 = scores(t, 0)
            s0 = jnp.concatenate([jnp.where(causal, s0[:BLK], -1e30), s0[BLK:]], axis=0)
            sbuf[t][rows(0), :] = s0
            tops.append(fold(jnp.max, s0))

        def score(j, ms):
            ss = [scores(t, j) for t in TWO]
            for t in TWO:
                sbuf[t][rows(j), :] = ss[t]
            return tuple(jnp.maximum(ms[t], fold(jnp.max, ss[t])) for t in TWO)
        tops = lax.fori_loop(1, chunks, score, tuple(tops))
        tops = [jnp.max(m, axis=0, keepdims=True) for m in tops]

        for t in TWO:
            ot[t][...] = jnp.zeros((HD + 16, W), F32)

        def forward(j, carry):
            es = [jnp.exp(sbuf[t][rows(j), :] - tops[t]) for t in TWO]
            for t in TWO:
                sbuf[t][rows(j), :] = es[t]
            for t in TWO:
                ot[t][...] += mm(jnp.concatenate([chunk(t, vc, j), ones], axis=1), es[t].astype(BF), TN)
            return carry
        lax.fori_loop(0, chunks, forward, 0)
        rls, deltas = [], []
        for t in TWO:
            rl = 1.0 / ot[t][HD:HD + 1, :]
            o_t = (ot[t][:HD, :] * rl).astype(BF).astype(F32)
            rls.append(rl)
            deltas.append(jnp.sum(o_t * dot_t[t].astype(F32), axis=0, keepdims=True))
            for g in range(G):
                part = slice(g * BLK, (g + 1) * BLK)
                attn_ref[pl.ds(bases[t], BLK), part] = o_t[:, part].T.astype(BF)

        def put(acc, t, i, term):
            slot = slots[bs[t], i]
            where = span(slot & 255)
            acc[where, :] += jnp.where(slot >= 256, term.astype(BF).astype(F32), term)

        for t in TWO:
            ot[t][:HD, :] = jnp.zeros((HD, W), F32)

        def backward(j, carry):
            terms = []
            for t in TWO:
                k, v = chunk(t, kc, j), chunk(t, vc, j)
                p = sbuf[t][rows(j), :] * rls[t]
                ds = (p * (mm(v, dot_t[t], NN) - deltas[t])).astype(BF)
                dv = mm(dot_t[t], p.astype(BF), NT)
                dk = mm(qs_t[t], ds, NT) * scaling
                ot[t][:HD, :] += mm(k, ds, TN)
                terms.append((dk, dv))
            for t in TWO:
                dk, dv = terms[t]
                for h in range(CHUNK):
                    put(ak, t, CHUNK * j + h, dk[:, h * BLK:(h + 1) * BLK])
                    put(av, t, CHUNK * j + h, dv[:, h * BLK:(h + 1) * BLK])
            return carry
        lax.fori_loop(0, chunks, backward, 0)
        for t in TWO:
            for g in range(G):
                part = slice(g * BLK, (g + 1) * BLK)
                dq_ref[pl.ds(bases[t], BLK), part] = (ot[t][:HD, part] * scaling).T.astype(BF)

    saves = [pltpu.make_async_copy(attn_ref, attn_hbm, sems.at[4]), pltpu.make_async_copy(dq_ref, dq_hbm, sems.at[5])]
    for copy in saves:
        copy.start()
    @pl.loop(0, NSEC)
    def _(s):
        @pl.when(done[s] == 1)
        def _():
            share = shares[s][:1]
            gk, gv = ak[span(NBLK + s), :] * share, av[span(NBLK + s), :] * share

            @pl.loop(first[s], stop[s])
            def _(c):
                ak[span(c), :] += gk
                av[span(c), :] += gv

    STEP = 4
    PARTS = 4

    for part in range(PARTS):
        size = NBLK // PARTS

        @pl.loop(part * size // STEP, (part + 1) * size // STEP)
        def _(i):
            at = pl.ds(pl.multiple_of(i * STEP * BLK, STEP * BLK), STEP * BLK)
            dk_ref[at, :] = ak[at, :].astype(BF)
            dv_ref[at, :] = av[at, :].astype(BF)
        at = pl.ds(part * size * BLK, size * BLK)
        for j, (src, dst) in enumerate(((dk_ref, dk_hbm), (dv_ref, dv_hbm))):
            copy = pltpu.make_async_copy(src.at[at, :], dst.at[at, :], sems.at[6 + 2 * part + j])
            copy.start()
            saves.append(copy)
    for copy in saves:
        copy.wait()


def attention(meta, q, k, v, do, NSEC=16, XR=12):
    NBLK = k.shape[0] // BLK
    NQ = q.shape[0] // BLK
    G = q.shape[1] // HD
    W = G * BLK
    slots_most = -(-(6 + XR) // CHUNK) * CHUNK
    hbm = pl.BlockSpec(memory_space=pltpu.HBM)
    every = ((NBLK + NSEC) * BLK, HD)
    return pl.pallas_call(
        functools.partial(attention_kernel, NBLK, NSEC, NQ, G, XR),
        out_shape=(jax.ShapeDtypeStruct(q.shape, BF), jax.ShapeDtypeStruct(q.shape, BF),
                   jax.ShapeDtypeStruct(k.shape, BF), jax.ShapeDtypeStruct(k.shape, BF)),
        in_specs=[pl.BlockSpec(memory_space=pltpu.SMEM)] + [hbm] * 4,
        out_specs=(hbm,) * 4,
        scratch_shapes=[
            pltpu.VMEM(every, BF),
            pltpu.VMEM(every, BF),
            pltpu.VMEM(every, F32),
            pltpu.VMEM(every, F32),
            pltpu.VMEM((slots_most * BLK, W), F32),
            pltpu.VMEM((slots_most * BLK, W), F32),
            pltpu.VMEM(q.shape, BF),
            pltpu.VMEM(q.shape, BF),
            pltpu.VMEM(q.shape, BF),
            pltpu.VMEM(q.shape, BF),
            pltpu.VMEM(k.shape, BF),
            pltpu.VMEM(k.shape, BF),
            pltpu.VMEM((BOTH, HD, W), BF),
            pltpu.VMEM((BOTH, HD, W), BF),
            pltpu.VMEM((HD + 16, W), F32),
            pltpu.VMEM((HD + 16, W), F32),
            pltpu.VMEM((NSEC, 8, HD), F32),
            pltpu.SMEM((NQ, 32), jnp.int32),
            pltpu.SMEM((NQ,), jnp.int32),
            pltpu.SMEM((NSEC,), jnp.int32),
            pltpu.SMEM((NSEC,), jnp.int32),
            pltpu.SMEM((NSEC,), jnp.int32),
            pltpu.SemaphoreType.DMA((16,)),
        ],
        compiler_params=pltpu.CompilerParams(vmem_limit_bytes=62 * 1024 * 1024),
        cost_estimate=pl.CostEstimate(flops=18_000_000_000, bytes_accessed=24_000_000, transcendentals=12_000_000),
    )(meta, q, k, v, do)


class Links:
    def __init__(self, send_sems, recv_sems):
        s = lax.axis_index("seq")
        self.y = lax.axis_index("head")
        self.x = s // 8
        self.z = (s // 2) % RING
        self.c = s % 2
        self.send_sems, self.recv_sems = send_sems, recv_sems
        self.used = 0
        self.sent = []

    def device(self, axis, step):
        x, z, y, c = self.x, self.z, self.y, self.c
        if axis == "x":
            x = (x + step) % RING
        elif axis == "z":
            z = (z + step) % RING
        elif axis == "y":
            y = (y + step) % RING
        else:
            c = 1 - c
        return ((x * RING + z) * 2 + c, y)

    def everyone(self):
        return [self.device(a, d) for a in "xzy" for d in (1, RING - 1)] + [self.device("c", 1)]

    def barrier(self):
        sem = pltpu.get_barrier_semaphore()
        for device in self.everyone():
            pl.semaphore_signal(sem, inc=1, device_id=device, device_id_type=MESH)
        pl.semaphore_wait(sem, 7)

    def number(self):
        self.used += 1
        return self.used - 1

    def send(self, number, src, dst, axis, step):
        copy = pltpu.make_async_remote_copy(
            src_ref=src, dst_ref=dst, send_sem=self.send_sems.at[number], recv_sem=self.recv_sems.at[number],
            device_id=self.device(axis, step), device_id_type=MESH)
        copy.start()
        self.sent.append(copy)

    def arrived(self, number, dst):
        pltpu.make_async_remote_copy(
            src_ref=dst, dst_ref=dst, send_sem=self.send_sems.at[number], recv_sem=self.recv_sems.at[number],
            device_id=self.device("c", 1), device_id_type=MESH).wait_recv()

    def finish(self):
        for copy in self.sent:
            copy.wait_send()


class Gather:
    def __init__(self, links, array, rows, pitch, offset, split, a, b):
        self.L, self.array, self.rows, self.pitch, self.offset, self.split = links, array, rows, pitch, offset, split
        self.a, self.b = a, b
        self.na = [links.number() for _ in range(4)]
        self.nb = [[links.number() for _ in range(4)] for _ in range(4)]

    def at(self, da, db, half=None):
        L = self.L
        move = {self.a: da, self.b: db}
        x, z = (L.x + move["x"]) % RING, (L.z + move["z"]) % RING
        start, count = self.offset, self.rows
        if half == 0:
            count = self.split
        elif half == 1:
            start, count = self.offset + self.split, self.rows - self.split
        return self.array.at[pl.ds(pl.multiple_of((x * RING + z) * self.pitch + start, 16), count), :]

    def put(self, number, axis, step, da, db, half=None):
        self.L.send(number, self.at(da, db, half), self.at(da, db, half), axis, step)

    def begin(self):
        self.put(self.na[0], self.a, 1, 0, 0)
        self.put(self.na[1], self.a, 3, 0, 0)

    def spread(self, i, da):
        self.put(self.nb[i][0], self.b, 1, da, 0)
        self.put(self.nb[i][1], self.b, 3, da, 0)

    def near(self):
        self.L.arrived(self.na[0], self.at(3, 0))
        self.put(self.na[2], self.a, 1, 3, 0, 0)
        self.L.arrived(self.na[1], self.at(1, 0))
        self.put(self.na[3], self.a, 3, 1, 0, 1)
        self.spread(0, 0)
        self.spread(1, 3)
        self.spread(2, 1)

    def far(self):
        self.L.arrived(self.na[2], self.at(2, 0, 0))
        self.L.arrived(self.na[3], self.at(2, 0, 1))
        self.spread(3, 2)

    def relay(self, i):
        da = (0, 3, 1, 2)[i]
        self.L.arrived(self.nb[i][0], self.at(da, 3))
        self.put(self.nb[i][2], self.b, 1, da, 3, 0)
        self.L.arrived(self.nb[i][1], self.at(da, 1))
        self.put(self.nb[i][3], self.b, 3, da, 1, 1)

    def end(self, i):
        da = (0, 3, 1, 2)[i]
        self.L.arrived(self.nb[i][2], self.at(da, 2, 0))
        self.L.arrived(self.nb[i][3], self.at(da, 2, 1))


def gather_kernel(q, k, v, wt, dp, meta, qh, kall, vall, wall, dattn, metas, wbuf, dbuf, abuf, send_sems, recv_sems, own_sems):
    L = Links(send_sems, recv_sems)
    chip = L.x * RING + L.z
    other = 1 - L.c
    T = k.shape[0]
    HD = kall.shape[1]
    W = qh.shape[1]
    C = wt.shape[0]
    D = dp.shape[1]
    L.barrier()

    pairs = []

    def split(src, width, dst, first, rows):
        at = dst.at[pl.ds(pl.multiple_of(first, 16), rows), :]
        pairs.append((L.number(), src, width, dst, at, rows))

    mine = chip * 2 * T + L.c * T
    split(wt, W, wbuf, chip * 2 * C + L.c * C, C)
    split(k, HD, kall, mine, T)
    split(v, HD, vall, mine, T)
    split(q, W, qh, L.c * T, T)
    own = []
    for i, (number, src, width, dst, at, rows) in enumerate(pairs):
        L.send(number, src.at[:, pl.ds(pl.multiple_of(other * width, 128), width)], at, "c", 1)
        copy = pltpu.make_async_copy(src.at[:, pl.ds(pl.multiple_of(L.c * width, 128), width)], at, own_sems.at[i])
        copy.start()
        own.append(copy)
    n_meta = L.number()
    mrow = metas.at[L.c]
    L.send(n_meta, meta, mrow, "c", 1)
    own_meta = pltpu.make_async_copy(meta, mrow, own_sems.at[4])
    own_meta.start()

    def piece(core, dy, half=None):
        ref = dbuf.at[core * RING + (L.y + dy) % RING]
        if half is None:
            return ref
        return ref.at[pl.ds(half * (T // 2), T // 2), :]

    ny = [L.number() for _ in range(4)]
    nc = [L.number() for _ in range(4)]
    L.send(ny[0], dp, piece(L.c, 0), "y", 1)
    L.send(ny[1], dp, piece(L.c, 0), "y", 3)
    L.send(nc[0], dp, piece(L.c, 0), "c", 1)
    own_d = pltpu.make_async_copy(dp, piece(L.c, 0), own_sems.at[5])
    own_d.start()

    sibling = [chip * 2 * C + other * C, chip * 2 * T + other * T, chip * 2 * T + other * T, other * T]

    def both(i):
        number, src, width, dst, at, rows = pairs[i]
        L.arrived(number, dst.at[pl.ds(pl.multiple_of(sibling[i], 16), rows), :])
        own[i].wait()

    first_w = (C // 2 + 15) // 16 * 16
    w0 = Gather(L, wbuf, C, 2 * C, 0, first_w, "x", "z")
    w1 = Gather(L, wbuf, C, 2 * C, C, first_w, "z", "x")
    gk = Gather(L, kall, 2 * T, 2 * T, 0, T, "x", "z")
    gv = Gather(L, vall, 2 * T, 2 * T, 0, T, "z", "x")
    both(0)
    w0.begin()
    w1.begin()
    both(1)
    gk.begin()
    both(2)
    gv.begin()
    w0.near()
    w1.near()
    gk.near()
    gv.near()
    w0.far()
    w1.far()
    gk.far()
    gv.far()
    L.arrived(ny[0], piece(L.c, 3))
    L.send(ny[2], piece(L.c, 3, 0), piece(L.c, 3, 0), "y", 1)
    L.arrived(ny[1], piece(L.c, 1))
    L.send(ny[3], piece(L.c, 1, 1), piece(L.c, 1, 1), "y", 3)
    L.send(nc[1], piece(L.c, 3), piece(L.c, 3), "c", 1)
    L.send(nc[2], piece(L.c, 1), piece(L.c, 1), "c", 1)
    for i in range(4):
        w0.relay(i)
        w1.relay(i)
    for i in range(2):
        gk.relay(i)
        gv.relay(i)
    L.arrived(ny[2], piece(L.c, 2, 0))
    L.arrived(ny[3], piece(L.c, 2, 1))
    L.send(nc[3], piece(L.c, 2), piece(L.c, 2), "c", 1)
    for i in range(4):
        w0.end(i)
        w1.end(i)
    keep = pltpu.make_async_copy(wbuf, wall, own_sems.at[6])
    keep.start()

    step = 256

    def product(core, t):
        rows = pl.ds(pl.multiple_of(t * step, step), step)
        total = jnp.zeros((step, W), F32)
        for y in range(RING):
            total += jnp.dot(dbuf[core * RING + y, rows, :], wbuf[y * D:(y + 1) * D, :], preferred_element_type=F32)
        abuf[pl.ds(pl.multiple_of(core * T + t * step, step), step), :] = total.astype(BF)

    def products(core):
        @pl.loop(0, T // step)
        def _(t):
            product(core, t)

    gk.relay(2)
    gv.relay(2)
    own_d.wait()
    products(L.c)
    gk.relay(3)
    gv.relay(3)
    for i, dy in enumerate((0, 3, 1, 2)):
        L.arrived(nc[i], piece(other, dy))
    products(other)
    save = pltpu.make_async_copy(abuf, dattn, own_sems.at[7])
    save.start()
    for i in range(4):
        gk.end(i)
        gv.end(i)
    both(3)
    L.arrived(n_meta, metas.at[other])
    own_meta.wait()
    keep.wait()
    save.wait()
    L.finish()


def gather(q, k, v, wt, dp, meta, seq):
    T = k.shape[0]
    HD = k.shape[1] // 2
    W = q.shape[1] // 2
    C = wt.shape[0]
    D = dp.shape[1]
    anywhere = pl.BlockSpec(memory_space=pltpu.HBM)
    sems = 128
    return pl.pallas_call(
        gather_kernel,
        out_shape=(
            jax.ShapeDtypeStruct((2 * T, W), BF),
            jax.ShapeDtypeStruct((seq * T, HD), BF),
            jax.ShapeDtypeStruct((seq * T, HD), BF),
            jax.ShapeDtypeStruct((seq * C, W), BF),
            jax.ShapeDtypeStruct((2 * T, W), BF),
            jax.ShapeDtypeStruct((2,) + meta.shape, jnp.int32),
        ),
        in_specs=[anywhere] * 6,
        out_specs=(anywhere,) * 6,
        scratch_shapes=[
            pltpu.VMEM((seq * C, W), BF),
            pltpu.VMEM((2 * RING, T, D), BF),
            pltpu.VMEM((2 * T, W), BF),
            pltpu.SemaphoreType.DMA((sems,)),
            pltpu.SemaphoreType.DMA((sems,)),
            pltpu.SemaphoreType.DMA((8,)),
        ],
        compiler_params=pltpu.CompilerParams(
            collective_id=0, has_side_effects=True, vmem_limit_bytes=40 * 1024 * 1024),
        cost_estimate=pl.CostEstimate(flops=3_400_000_000, bytes_accessed=40_000_000, transcendentals=0),
    )(q, k, v, wt, dp, meta)


class Scatter:
    def __init__(self, links, source, buf, far, near, far2, near2, final, a, b, load_sem):
        self.L, self.source, self.buf = links, source, buf
        self.farr, self.nearr, self.far2, self.near2, self.final = far, near, far2, near2, final
        self.a, self.b = a, b
        self.rows = final.shape[0]
        self.nb = [[links.number() for _ in range(4)] for _ in range(4)]
        self.na = [links.number() for _ in range(4)]
        self.load = pltpu.make_async_copy(source, buf, load_sem)
        self.load.start()

    def where(self, da, db, half=None):
        L = self.L
        move = {self.a: da, self.b: db}
        x, z = (L.x + move["x"]) % RING, (L.z + move["z"]) % RING
        start, count = 0, self.rows
        if half is not None:
            count = self.rows // 2
            start = half * count
        return pl.ds(pl.multiple_of((x * RING + z) * self.rows + start, 16), count)

    def half(self, h):
        return pl.ds(h * (self.rows // 2), self.rows // 2)

    def begin(self, i):
        da = (2, 3, 1, 0)[i]
        for h, step in ((0, 1), (1, 3)):
            self.L.send(self.nb[i][h], self.source.at[self.where(da, 2, h), :], self.farr.at[i, h], self.b, step)

    def loaded(self):
        self.load.wait()

    def pass_on(self, i):
        da = (2, 3, 1, 0)[i]
        for h, step in ((0, 1), (1, 3)):
            self.L.arrived(self.nb[i][h], self.farr.at[i, h])
            at = self.where(da, step, h)
            self.buf[at, :] = (self.buf[at, :].astype(F32) + self.farr[i, h].astype(F32)).astype(BF)
            self.L.send(self.nb[i][2 + h], self.buf.at[self.where(da, step), :], self.nearr.at[i, h], self.b, step)

    def total(self, i, da, h):
        at = self.where(da, 0, h)
        part = self.half(h)
        return (self.buf[at, :].astype(F32) + self.nearr[i, 0, part, :].astype(F32)
                + self.nearr[i, 1, part, :].astype(F32))

    def close(self, i):
        da = (2, 3, 1, 0)[i]
        for h in range(2):
            self.L.arrived(self.nb[i][2 + h], self.nearr.at[i, h])
        if i == 0:
            for h, step in ((0, 1), (1, 3)):
                at = self.where(da, 0, h)
                self.buf[at, :] = self.total(i, da, h).astype(BF)
                self.L.send(self.na[h], self.buf.at[at, :], self.far2.at[h], self.a, step)
        elif i < 3:
            take = 1 if da == 3 else 0
            self.L.arrived(self.na[take], self.far2.at[take])
            for h in range(2):
                value = self.total(i, da, h)
                if h == take:
                    value += self.far2[take].astype(F32)
                self.buf[self.where(da, 0, h), :] = value.astype(BF)
            self.L.send(self.na[2 + take], self.buf.at[self.where(da, 0), :], self.near2.at[take], self.a, da)

    def finish(self):
        for take in range(2):
            self.L.arrived(self.na[2 + take], self.near2.at[take])
        for h in range(2):
            part = self.half(h)
            value = (self.total(3, 0, h) + self.near2[0, part, :].astype(F32)
                     + self.near2[1, part, :].astype(F32))
            self.final[part, :] = jnp.concatenate(
                [value[i:i + BLK].T for i in range(0, value.shape[0], BLK)], axis=0).astype(BF)


def scatter_kernel(dk, dv, attn, wall, dq, proj, dqo, dko, dvo,
                   bufk, bufv, farr, nearr, far2, near2, final, there, here, halves, wholes, result,
                   send_sems, recv_sems, own_sems):
    L = Links(send_sems, recv_sems)
    other = 1 - L.c
    T = proj.shape[0]
    D = proj.shape[1]
    W = dq.shape[1]
    HD = dk.shape[1]
    L.barrier()
    sk = Scatter(L, dk, bufk, farr.at[0], nearr.at[0], far2.at[0], near2.at[0], final.at[0], "x", "z", own_sems.at[0])
    sv = Scatter(L, dv, bufv, farr.at[1], nearr.at[1], far2.at[1], near2.at[1], final.at[1], "z", "x", own_sems.at[1])
    for i in range(2):
        sk.begin(i)
        sv.begin(i)

    def rows_of(core):
        return pl.ds(pl.multiple_of(core * T, 16), T)

    def heads(ref, core, width):
        return ref.at[:, pl.ds(pl.multiple_of(core * width, 128), width)]

    n_q = L.number()
    L.send(n_q, dq.at[rows_of(other), :], heads(dqo, L.c, W), "c", 1)
    own_q = pltpu.make_async_copy(dq.at[rows_of(L.c), :], heads(dqo, L.c, W), own_sems.at[2])
    own_q.start()

    n_there = [L.number() for _ in range(4)]
    ny = [L.number() for _ in range(4)]
    order = (2, 1, 3, 0)

    def product(core, dy):
        y = (L.y + dy) % RING
        w = wall[pl.ds(pl.multiple_of(y * D, 16), D), :]
        return lax.dot_general(attn[rows_of(core), :], w, (((1,), (1,)), ((), ())), preferred_element_type=F32)

    def away(i):
        here[i] = product(other, order[i]).astype(BF)
        L.send(n_there[i], here.at[i], there.at[i], "c", 1)

    def mine(i):
        value = product(L.c, order[i])
        L.arrived(n_there[i], there.at[i])
        return value + there[i].astype(F32)

    mid = T // 2
    away(0)
    sk.loaded()
    sv.loaded()
    sk.pass_on(0)
    sv.pass_on(0)
    sk.begin(2)
    sv.begin(2)
    away(1)
    sk.pass_on(1)
    sv.pass_on(1)
    sk.begin(3)
    sv.begin(3)
    away(2)
    sk.close(0)
    sv.close(0)
    away(3)
    sk.pass_on(2)
    sv.pass_on(2)
    result[0] = mine(0).astype(BF)
    L.send(ny[0], result.at[0, pl.ds(0, mid), :], halves.at[0], "y", 1)
    L.send(ny[1], result.at[0, pl.ds(mid, mid), :], halves.at[1], "y", 3)
    sk.close(1)
    sv.close(1)
    sk.pass_on(3)
    sv.pass_on(3)
    value = mine(1)
    L.arrived(ny[0], halves.at[0])
    result[1] = jnp.concatenate([value[:mid] + halves[0].astype(F32), value[mid:]], axis=0).astype(BF)
    L.send(ny[2], result.at[1], wholes.at[0], "y", 1)
    value = mine(2)
    L.arrived(ny[1], halves.at[1])
    result[2] = jnp.concatenate([value[:mid], value[mid:] + halves[1].astype(F32)], axis=0).astype(BF)
    L.send(ny[3], result.at[2], wholes.at[1], "y", 3)
    sk.close(2)
    sv.close(2)
    value = mine(3)
    L.arrived(ny[2], wholes.at[0])
    L.arrived(ny[3], wholes.at[1])
    result[3] = (value + wholes[0].astype(F32) + wholes[1].astype(F32)).astype(BF)
    own_p = pltpu.make_async_copy(result.at[3], proj, own_sems.at[3])
    own_p.start()
    outs = []
    for j, (s, out) in enumerate(((sk, dko), (sv, dvo))):
        s.close(3)
        s.finish()
        n = L.number()
        L.send(n, final.at[j, rows_of(other), :], heads(out, L.c, HD), "c", 1)
        own = pltpu.make_async_copy(final.at[j, rows_of(L.c), :], heads(out, L.c, HD), own_sems.at[4 + j])
        own.start()
        outs.append((n, out, own))
    L.arrived(n_q, heads(dqo, other, W))
    own_q.wait()
    own_p.wait()
    for n, out, own in outs:
        L.arrived(n, heads(out, other, HD))
        own.wait()
    L.finish()


def scatter(dk, dv, attn, wall, dq, D):
    T = dq.shape[0] // 2
    W = dq.shape[1]
    HD = dk.shape[1]
    anywhere = pl.BlockSpec(memory_space=pltpu.HBM)
    vmem = pl.BlockSpec(memory_space=pltpu.VMEM)
    sems = 64
    return pl.pallas_call(
        scatter_kernel,
        out_shape=(
            jax.ShapeDtypeStruct((T, D), BF),
            jax.ShapeDtypeStruct((T, 2 * W), BF),
            jax.ShapeDtypeStruct((T, 2 * HD), BF),
            jax.ShapeDtypeStruct((T, 2 * HD), BF),
        ),
        in_specs=[anywhere, anywhere, vmem, vmem, anywhere],
        out_specs=(anywhere,) * 4,
        scratch_shapes=[
            pltpu.VMEM(dk.shape, BF),
            pltpu.VMEM(dk.shape, BF),
            pltpu.VMEM((2, 4, 2, T, HD), BF),
            pltpu.VMEM((2, 4, 2, 2 * T, HD), BF),
            pltpu.VMEM((2, 2, T, HD), BF),
            pltpu.VMEM((2, 2, 2 * T, HD), BF),
            pltpu.VMEM((2, 2 * T, HD), BF),
            pltpu.VMEM((4, T, D), BF),
            pltpu.VMEM((4, T, D), BF),
            pltpu.VMEM((2, T // 2, D), BF),
            pltpu.VMEM((2, T, D), BF),
            pltpu.VMEM((4, T, D), BF),
            pltpu.SemaphoreType.DMA((sems,)),
            pltpu.SemaphoreType.DMA((sems,)),
            pltpu.SemaphoreType.DMA((6,)),
        ],
        compiler_params=pltpu.CompilerParams(
            collective_id=1, has_side_effects=True, vmem_limit_bytes=56 * 1024 * 1024),
        cost_estimate=pl.CostEstimate(flops=3_400_000_000, bytes_accessed=40_000_000, transcendentals=0),
    )(dk, dv, attn, wall, dq)


def on_device(queries, keys, values, out_weight, d_proj, block_section, section_parent, xref_owner, xref_block, xref_valid):
    seq = lax.axis_size("seq")
    blocks, xrefs = xref_block.shape
    target = jnp.where(xref_valid > 0, xref_owner.reshape(blocks, xrefs) * blocks + xref_block, -1)
    first = (lax.axis_index("seq") // 2) * 2 * blocks
    meta = jnp.concatenate([
        jnp.pad(target, ((0, 0), (0, 128 - xrefs))),
        block_section[None, :],
        jnp.pad(section_parent, (0, 128 - section_parent.shape[0]))[None, :],
        jnp.full((2, 128), first, jnp.int32),
    ], axis=0)
    qh, kall, vall, wall, d_attn, metas = gather(queries, keys, values, out_weight.T, d_proj, meta, seq)
    attn, dq, dk, dv = attention(metas.reshape(16, 128), qh, kall, vall, d_attn)
    return scatter(dk, dv, attn, wall, dq, d_proj.shape[1])


def solution(mesh):
    split = P("seq", "head")
    rows = P("seq", None)
    return jax.shard_map(
        on_device, mesh=mesh,
        in_specs=(split, split, split, P("head", "seq"), split, P(), P(), rows, rows, rows),
        out_specs=(split,) * 4, check_vma=False)
```

```python
import functools
import jax, jax.numpy as jnp
from jax import lax
from jax.experimental import pallas as pl
from jax.experimental.pallas import tpu as pltpu
from jax.sharding import PartitionSpec as P
F32, BF = jnp.float32, jnp.bfloat16
MESH = pl.DeviceIdType.MESH
RING = 4


HD = 128
BLK = 128
CHUNK = 4
BOTH = 2


def attention_kernel(NBLK, NSEC, NQ, G, XR, sec_hbm, par_hbm, xo_hbm, xb_hbm, xv_hbm, q_hbm, k_hbm, v_hbm, do_hbm, attn_hbm, dq_hbm, dk_hbm, dv_hbm,
                     kc, vc, ak, av, sbuf0, sbuf1, q_ref, do_ref, attn_ref, dq_ref, dk_ref, dv_ref,
                     qs_t, dot_t, ot0, ot1, shares, slots, counts, first, stop, done, sec, parent, xo, xb, xv, sems):
    scaling = HD ** -0.5
    sbuf, ot = (sbuf0, sbuf1), (ot0, ot1)
    NT = (((1,), (1,)), ((), ()))
    TN = (((0,), (0,)), ((), ()))
    NN = (((1,), (0,)), ((), ()))
    R = CHUNK * BLK

    def mm(a, b, dims):
        return lax.dot_general(a, b, dims, preferred_element_type=F32)

    loads = [pltpu.make_async_copy(src, dst, sems.at[i]) for i, (src, dst) in enumerate((
        (k_hbm, kc.at[pl.ds(0, NBLK * BLK)]), (v_hbm, vc.at[pl.ds(0, NBLK * BLK)]), (q_hbm, q_ref), (do_hbm, do_ref)))]
    tables = [pltpu.make_async_copy(src, dst, sems.at[16 + i]) for i, (src, dst) in enumerate((
        (sec_hbm, sec), (par_hbm, parent), (xo_hbm, xo), (xb_hbm, xb), (xv_hbm, xv)))]
    for copy in tables + loads:
        copy.start()
    for copy in tables:
        copy.wait()
    begin = (lax.axis_index("seq") // 2) * NQ

    @pl.loop(0, NSEC)
    def _(s):
        stop[s] = 0
        first[s] = 0
        done[s] = 0

    @pl.loop(0, NBLK // 8)
    def _(i):
        for h in range(8):
            c = i * 8 + h
            stop[sec[c]] = c + 1
            d = NBLK - 1 - c
            first[sec[d]] = d

    @pl.loop(0, NQ)
    def _(b):
        g = begin + b
        mine = sec[g]
        for j in range(32):
            slots[b, j] = g
        slots[b, 1] = NBLK + mine
        n = jnp.int32(2)
        for w in (1, 2, 3):
            c = g - w
            cs = jnp.maximum(c, 0)
            slots[b, n] = cs
            n = n + jnp.where((c >= 0) & (sec[cs] == mine), 1, 0)
        up = parent[mine]
        slots[b, n] = NBLK + jnp.maximum(up, 0)
        n = n + jnp.where(up >= 0, 1, 0)
        core, row = lax.div(b, NQ // 2), lax.rem(b, NQ // 2)
        for j in range(XR):
            slots[b, n] = xo[core, row * XR + j, 0] * (NQ // 2) + xb[core, row, j] + 256
            n = n + jnp.where(xv[core, row, j] > 0, 1, 0)
        slots[b, n] = g
        counts[b] = n

    @pl.loop(0, (NBLK + NSEC) // 4)
    def _(i):
        at = pl.ds(pl.multiple_of(i * 512, 512), 512)
        ak[at, :] = jnp.zeros((512, HD), F32)
        av[at, :] = jnp.zeros((512, HD), F32)

    for copy in loads:
        copy.wait()

    def span(i):
        return pl.ds(pl.multiple_of(i * BLK, BLK), BLK)

    def summarize(s):
        def add(c, t):
            return t[0] + kc[span(c), :].astype(F32), t[1] + vc[span(c), :].astype(F32)
        zero = jnp.zeros((BLK, HD), F32)
        tk, tv = lax.fori_loop(first[s], stop[s], add, (zero, zero))
        share = 1.0 / jnp.sqrt(jnp.full((8, HD), jnp.maximum(stop[s] - first[s], 1)).astype(F32))
        shares[s] = share
        kc[span(NBLK + s), :] = (tk * share[:1]).astype(BF)
        vc[span(NBLK + s), :] = (tv * share[:1]).astype(BF)
        done[s] = 1

    @pl.loop(0, 2 * NQ)
    def _(i):
        mine = sec[begin + lax.div(i, 2)]
        s = jnp.where(lax.rem(i, 2) == 0, mine, jnp.maximum(parent[mine], 0))

        @pl.when(done[s] == 0)
        def _():
            summarize(s)

    W = G * BLK
    row_id = lax.broadcasted_iota(jnp.int32, (BLK, BLK), 0)
    col_id = lax.broadcasted_iota(jnp.int32, (BLK, BLK), 1)
    causal = jnp.concatenate([row_id <= col_id] * G, axis=1)

    def fold(op, s):
        return op(s.reshape(s.shape[0] // 8, 8, W), axis=0)

    ones = jnp.ones((R, 16), BF)

    TWO = range(BOTH)

    @pl.loop(0, NQ // BOTH)
    def _(u):
        bs = [u * BOTH + t for t in TWO]
        bases = [pl.multiple_of(b * BLK, BLK) for b in bs]
        for t in TWO:
            for g in range(G):
                part = slice(g * BLK, (g + 1) * BLK)
                qs_t[t, :, part] = q_ref[pl.ds(bases[t], BLK), part].astype(F32).T.astype(BF)
                dot_t[t, :, part] = do_ref[pl.ds(bases[t], BLK), part].astype(F32).T.astype(BF)
        ns = [counts[b] for b in bs]
        most = ns[0]
        for n in ns[1:]:
            most = jnp.maximum(most, n)
        chunks = lax.div(most + CHUNK - 1, CHUNK)

        def chunk(t, ref, j):
            return jnp.concatenate([ref[span(slots[bs[t], CHUNK * j + h] & 255), :] for h in range(CHUNK)], axis=0)

        def rows(j):
            return pl.ds(pl.multiple_of(j * R, R), R)

        def scores(t, j):
            s = mm(chunk(t, kc, j), qs_t[t], NN) * scaling
            return jnp.concatenate([
                s[h * BLK:(h + 1) * BLK] + jnp.where(CHUNK * j + h < ns[t], 0.0, -1e30) for h in range(CHUNK)], axis=0)

        tops = []
        for t in TWO:
            s0 = scores(t, 0)
            s0 = jnp.concatenate([jnp.where(causal, s0[:BLK], -1e30), s0[BLK:]], axis=0)
            sbuf[t][rows(0), :] = s0
            tops.append(fold(jnp.max, s0))

        def score(j, ms):
            ss = [scores(t, j) for t in TWO]
            for t in TWO:
                sbuf[t][rows(j), :] = ss[t]
            return tuple(jnp.maximum(ms[t], fold(jnp.max, ss[t])) for t in TWO)
        tops = lax.fori_loop(1, chunks, score, tuple(tops))
        tops = [jnp.max(m, axis=0, keepdims=True) for m in tops]

        for t in TWO:
            ot[t][...] = jnp.zeros((HD + 16, W), F32)

        def forward(j, carry):
            es = [jnp.exp(sbuf[t][rows(j), :] - tops[t]) for t in TWO]
            for t in TWO:
                sbuf[t][rows(j), :] = es[t]
            for t in TWO:
                ot[t][...] += mm(jnp.concatenate([chunk(t, vc, j), ones], axis=1), es[t].astype(BF), TN)
            return carry
        lax.fori_loop(0, chunks, forward, 0)
        rls, deltas = [], []
        for t in TWO:
            rl = 1.0 / ot[t][HD:HD + 1, :]
            o_t = (ot[t][:HD, :] * rl).astype(BF).astype(F32)
            rls.append(rl)
            deltas.append(jnp.sum(o_t * dot_t[t].astype(F32), axis=0, keepdims=True))
            for g in range(G):
                part = slice(g * BLK, (g + 1) * BLK)
                attn_ref[pl.ds(bases[t], BLK), part] = o_t[:, part].T.astype(BF)

        def put(acc, t, i, term):
            slot = slots[bs[t], i]
            where = span(slot & 255)
            acc[where, :] += jnp.where(slot >= 256, term.astype(BF).astype(F32), term)

        for t in TWO:
            ot[t][:HD, :] = jnp.zeros((HD, W), F32)

        def backward(j, carry):
            terms = []
            for t in TWO:
                k, v = chunk(t, kc, j), chunk(t, vc, j)
                p = sbuf[t][rows(j), :] * rls[t]
                ds = (p * (mm(v, dot_t[t], NN) - deltas[t])).astype(BF)
                dv = mm(dot_t[t], p.astype(BF), NT)
                dk = mm(qs_t[t], ds, NT) * scaling
                ot[t][:HD, :] += mm(k, ds, TN)
                terms.append((dk, dv))
            for t in TWO:
                dk, dv = terms[t]
                for h in range(CHUNK):
                    put(ak, t, CHUNK * j + h, dk[:, h * BLK:(h + 1) * BLK])
                    put(av, t, CHUNK * j + h, dv[:, h * BLK:(h + 1) * BLK])
            return carry
        lax.fori_loop(0, chunks, backward, 0)
        for t in TWO:
            for g in range(G):
                part = slice(g * BLK, (g + 1) * BLK)
                dq_ref[pl.ds(bases[t], BLK), part] = (ot[t][:HD, part] * scaling).T.astype(BF)

    saves = [pltpu.make_async_copy(attn_ref, attn_hbm, sems.at[4]), pltpu.make_async_copy(dq_ref, dq_hbm, sems.at[5])]
    for copy in saves:
        copy.start()
    @pl.loop(0, NSEC)
    def _(s):
        @pl.when(done[s] == 1)
        def _():
            share = shares[s][:1]
            gk, gv = ak[span(NBLK + s), :] * share, av[span(NBLK + s), :] * share

            @pl.loop(first[s], stop[s])
            def _(c):
                ak[span(c), :] += gk
                av[span(c), :] += gv

    STEP = 4
    PARTS = 4

    for part in range(PARTS):
        size = NBLK // PARTS

        @pl.loop(part * size // STEP, (part + 1) * size // STEP)
        def _(i):
            at = pl.ds(pl.multiple_of(i * STEP * BLK, STEP * BLK), STEP * BLK)
            dk_ref[at, :] = ak[at, :].astype(BF)
            dv_ref[at, :] = av[at, :].astype(BF)
        at = pl.ds(part * size * BLK, size * BLK)
        for j, (src, dst) in enumerate(((dk_ref, dk_hbm), (dv_ref, dv_hbm))):
            copy = pltpu.make_async_copy(src.at[at, :], dst.at[at, :], sems.at[6 + 2 * part + j])
            copy.start()
            saves.append(copy)
    for copy in saves:
        copy.wait()


def attention(block_section, section_parent, xrefs, q, k, v, do):
    NSEC = section_parent.shape[0]
    XR = xrefs[1].shape[2]
    NBLK = k.shape[0] // BLK
    NQ = q.shape[0] // BLK
    G = q.shape[1] // HD
    W = G * BLK
    slots_most = -(-(6 + XR) // CHUNK) * CHUNK
    hbm = pl.BlockSpec(memory_space=pltpu.HBM)
    every = ((NBLK + NSEC) * BLK, HD)
    return pl.pallas_call(
        functools.partial(attention_kernel, NBLK, NSEC, NQ, G, XR),
        out_shape=(jax.ShapeDtypeStruct(q.shape, BF), jax.ShapeDtypeStruct(q.shape, BF),
                   jax.ShapeDtypeStruct(k.shape, BF), jax.ShapeDtypeStruct(k.shape, BF)),
        in_specs=[hbm] * 9,
        out_specs=(hbm,) * 4,
        scratch_shapes=[
            pltpu.VMEM(every, BF),
            pltpu.VMEM(every, BF),
            pltpu.VMEM(every, F32),
            pltpu.VMEM(every, F32),
            pltpu.VMEM((slots_most * BLK, W), F32),
            pltpu.VMEM((slots_most * BLK, W), F32),
            pltpu.VMEM(q.shape, BF),
            pltpu.VMEM(q.shape, BF),
            pltpu.VMEM(q.shape, BF),
            pltpu.VMEM(q.shape, BF),
            pltpu.VMEM(k.shape, BF),
            pltpu.VMEM(k.shape, BF),
            pltpu.VMEM((BOTH, HD, W), BF),
            pltpu.VMEM((BOTH, HD, W), BF),
            pltpu.VMEM((HD + 16, W), F32),
            pltpu.VMEM((HD + 16, W), F32),
            pltpu.VMEM((NSEC, 8, HD), F32),
            pltpu.SMEM((NQ, 32), jnp.int32),
            pltpu.SMEM((NQ,), jnp.int32),
            pltpu.SMEM((NSEC,), jnp.int32),
            pltpu.SMEM((NSEC,), jnp.int32),
            pltpu.SMEM((NSEC,), jnp.int32),
            pltpu.SMEM(block_section.shape, jnp.int32),
            pltpu.SMEM(section_parent.shape, jnp.int32),
        ] + [pltpu.SMEM(a.shape, jnp.int32) for a in xrefs] + [
            pltpu.SemaphoreType.DMA((24,)),
        ],
        compiler_params=pltpu.CompilerParams(vmem_limit_bytes=62 * 1024 * 1024),
        cost_estimate=pl.CostEstimate(flops=18_000_000_000, bytes_accessed=24_000_000, transcendentals=12_000_000),
    )(block_section, section_parent, *xrefs, q, k, v, do)


class Links:
    def __init__(self, send_sems, recv_sems):
        s = lax.axis_index("seq")
        self.y = lax.axis_index("head")
        self.x = s // 8
        self.z = (s // 2) % RING
        self.c = s % 2
        self.send_sems, self.recv_sems = send_sems, recv_sems
        self.used = 0
        self.sent = []

    def device(self, axis, step):
        x, z, y, c = self.x, self.z, self.y, self.c
        if axis == "x":
            x = (x + step) % RING
        elif axis == "z":
            z = (z + step) % RING
        elif axis == "y":
            y = (y + step) % RING
        else:
            c = 1 - c
        return ((x * RING + z) * 2 + c, y)

    def everyone(self):
        return [self.device(a, d) for a in "xzy" for d in (1, RING - 1)] + [self.device("c", 1)]

    def barrier(self):
        sem = pltpu.get_barrier_semaphore()
        for device in self.everyone():
            pl.semaphore_signal(sem, inc=1, device_id=device, device_id_type=MESH)
        pl.semaphore_wait(sem, 7)

    def number(self):
        self.used += 1
        return self.used - 1

    def send(self, number, src, dst, axis, step):
        copy = pltpu.make_async_remote_copy(
            src_ref=src, dst_ref=dst, send_sem=self.send_sems.at[number], recv_sem=self.recv_sems.at[number],
            device_id=self.device(axis, step), device_id_type=MESH)
        copy.start()
        self.sent.append(copy)

    def arrived(self, number, dst):
        pltpu.make_async_remote_copy(
            src_ref=dst, dst_ref=dst, send_sem=self.send_sems.at[number], recv_sem=self.recv_sems.at[number],
            device_id=self.device("c", 1), device_id_type=MESH).wait_recv()

    def finish(self):
        for copy in self.sent:
            copy.wait_send()


class Gather:
    def __init__(self, links, array, rows, pitch, offset, split, a, b):
        self.L, self.array, self.rows, self.pitch, self.offset, self.split = links, array, rows, pitch, offset, split
        self.a, self.b = a, b
        self.na = [links.number() for _ in range(4)]
        self.nb = [[links.number() for _ in range(4)] for _ in range(4)]

    def at(self, da, db, half=None):
        L = self.L
        move = {self.a: da, self.b: db}
        x, z = (L.x + move["x"]) % RING, (L.z + move["z"]) % RING
        start, count = self.offset, self.rows
        if half == 0:
            count = self.split
        elif half == 1:
            start, count = self.offset + self.split, self.rows - self.split
        return self.array.at[pl.ds(pl.multiple_of((x * RING + z) * self.pitch + start, 16), count), :]

    def put(self, number, axis, step, da, db, half=None):
        self.L.send(number, self.at(da, db, half), self.at(da, db, half), axis, step)

    def begin(self):
        self.put(self.na[0], self.a, 1, 0, 0)
        self.put(self.na[1], self.a, 3, 0, 0)

    def spread(self, i, da):
        self.put(self.nb[i][0], self.b, 1, da, 0)
        self.put(self.nb[i][1], self.b, 3, da, 0)

    def near(self):
        self.L.arrived(self.na[0], self.at(3, 0))
        self.put(self.na[2], self.a, 1, 3, 0, 0)
        self.L.arrived(self.na[1], self.at(1, 0))
        self.put(self.na[3], self.a, 3, 1, 0, 1)
        self.spread(0, 0)
        self.spread(1, 3)
        self.spread(2, 1)

    def far(self):
        self.L.arrived(self.na[2], self.at(2, 0, 0))
        self.L.arrived(self.na[3], self.at(2, 0, 1))
        self.spread(3, 2)

    def relay(self, i):
        da = (0, 3, 1, 2)[i]
        self.L.arrived(self.nb[i][0], self.at(da, 3))
        self.put(self.nb[i][2], self.b, 1, da, 3, 0)
        self.L.arrived(self.nb[i][1], self.at(da, 1))
        self.put(self.nb[i][3], self.b, 3, da, 1, 1)

    def end(self, i):
        da = (0, 3, 1, 2)[i]
        self.L.arrived(self.nb[i][2], self.at(da, 2, 0))
        self.L.arrived(self.nb[i][3], self.at(da, 2, 1))


def gather_kernel(q, k, v, wt, dp, xo, xb, xv, qh, kall, vall, wall, dattn, xos, xbs, xvs, wbuf, dbuf, abuf, send_sems, recv_sems, own_sems):
    L = Links(send_sems, recv_sems)
    chip = L.x * RING + L.z
    other = 1 - L.c
    T = k.shape[0]
    HD = kall.shape[1]
    W = qh.shape[1]
    C = wt.shape[0]
    D = dp.shape[1]
    L.barrier()

    pairs = []

    def split(src, width, dst, first, rows):
        at = dst.at[pl.ds(pl.multiple_of(first, 16), rows), :]
        pairs.append((L.number(), src, width, dst, at, rows))

    mine = chip * 2 * T + L.c * T
    split(wt, W, wbuf, chip * 2 * C + L.c * C, C)
    split(k, HD, kall, mine, T)
    split(v, HD, vall, mine, T)
    split(q, W, qh, L.c * T, T)
    own = []
    for i, (number, src, width, dst, at, rows) in enumerate(pairs):
        L.send(number, src.at[:, pl.ds(pl.multiple_of(other * width, 128), width)], at, "c", 1)
        copy = pltpu.make_async_copy(src.at[:, pl.ds(pl.multiple_of(L.c * width, 128), width)], at, own_sems.at[i])
        copy.start()
        own.append(copy)
    refs = []
    for i, (src, dst) in enumerate(((xo, xos), (xb, xbs), (xv, xvs))):
        n = L.number()
        L.send(n, src, dst.at[L.c], "c", 1)
        copy = pltpu.make_async_copy(src, dst.at[L.c], own_sems.at[8 + i])
        copy.start()
        refs.append((n, dst, copy))

    def piece(core, dy, half=None):
        ref = dbuf.at[core * RING + (L.y + dy) % RING]
        if half is None:
            return ref
        return ref.at[pl.ds(half * (T // 2), T // 2), :]

    ny = [L.number() for _ in range(4)]
    nc = [L.number() for _ in range(4)]
    L.send(ny[0], dp, piece(L.c, 0), "y", 1)
    L.send(ny[1], dp, piece(L.c, 0), "y", 3)
    L.send(nc[0], dp, piece(L.c, 0), "c", 1)
    own_d = pltpu.make_async_copy(dp, piece(L.c, 0), own_sems.at[5])
    own_d.start()

    sibling = [chip * 2 * C + other * C, chip * 2 * T + other * T, chip * 2 * T + other * T, other * T]

    def both(i):
        number, src, width, dst, at, rows = pairs[i]
        L.arrived(number, dst.at[pl.ds(pl.multiple_of(sibling[i], 16), rows), :])
        own[i].wait()

    first_w = (C // 2 + 15) // 16 * 16
    w0 = Gather(L, wbuf, C, 2 * C, 0, first_w, "x", "z")
    w1 = Gather(L, wbuf, C, 2 * C, C, first_w, "z", "x")
    gk = Gather(L, kall, 2 * T, 2 * T, 0, T, "x", "z")
    gv = Gather(L, vall, 2 * T, 2 * T, 0, T, "z", "x")
    both(0)
    w0.begin()
    w1.begin()
    both(1)
    gk.begin()
    both(2)
    gv.begin()
    w0.near()
    w1.near()
    gk.near()
    gv.near()
    w0.far()
    w1.far()
    gk.far()
    gv.far()
    L.arrived(ny[0], piece(L.c, 3))
    L.send(ny[2], piece(L.c, 3, 0), piece(L.c, 3, 0), "y", 1)
    L.arrived(ny[1], piece(L.c, 1))
    L.send(ny[3], piece(L.c, 1, 1), piece(L.c, 1, 1), "y", 3)
    L.send(nc[1], piece(L.c, 3), piece(L.c, 3), "c", 1)
    L.send(nc[2], piece(L.c, 1), piece(L.c, 1), "c", 1)
    for i in range(4):
        w0.relay(i)
        w1.relay(i)
    for i in range(2):
        gk.relay(i)
        gv.relay(i)
    L.arrived(ny[2], piece(L.c, 2, 0))
    L.arrived(ny[3], piece(L.c, 2, 1))
    L.send(nc[3], piece(L.c, 2), piece(L.c, 2), "c", 1)
    for i in range(4):
        w0.end(i)
        w1.end(i)
    keep = pltpu.make_async_copy(wbuf, wall, own_sems.at[6])
    keep.start()

    step = 256

    def product(core, t):
        rows = pl.ds(pl.multiple_of(t * step, step), step)
        total = jnp.zeros((step, W), F32)
        for y in range(RING):
            total += jnp.dot(dbuf[core * RING + y, rows, :], wbuf[y * D:(y + 1) * D, :], preferred_element_type=F32)
        abuf[pl.ds(pl.multiple_of(core * T + t * step, step), step), :] = total.astype(BF)

    def products(core):
        @pl.loop(0, T // step)
        def _(t):
            product(core, t)

    gk.relay(2)
    gv.relay(2)
    own_d.wait()
    products(L.c)
    gk.relay(3)
    gv.relay(3)
    for i, dy in enumerate((0, 3, 1, 2)):
        L.arrived(nc[i], piece(other, dy))
    products(other)
    save = pltpu.make_async_copy(abuf, dattn, own_sems.at[7])
    save.start()
    for i in range(4):
        gk.end(i)
        gv.end(i)
    both(3)
    for n, dst, copy in refs:
        L.arrived(n, dst.at[other])
        copy.wait()
    keep.wait()
    save.wait()
    L.finish()


def gather(q, k, v, wt, dp, xrefs, seq):
    T = k.shape[0]
    HD = k.shape[1] // 2
    W = q.shape[1] // 2
    C = wt.shape[0]
    D = dp.shape[1]
    anywhere = pl.BlockSpec(memory_space=pltpu.HBM)
    sems = 128
    return pl.pallas_call(
        gather_kernel,
        out_shape=(
            jax.ShapeDtypeStruct((2 * T, W), BF),
            jax.ShapeDtypeStruct((seq * T, HD), BF),
            jax.ShapeDtypeStruct((seq * T, HD), BF),
            jax.ShapeDtypeStruct((seq * C, W), BF),
            jax.ShapeDtypeStruct((2 * T, W), BF),
        ) + tuple(jax.ShapeDtypeStruct((2,) + a.shape, jnp.int32) for a in xrefs),
        in_specs=[anywhere] * 8,
        out_specs=(anywhere,) * 8,
        scratch_shapes=[
            pltpu.VMEM((seq * C, W), BF),
            pltpu.VMEM((2 * RING, T, D), BF),
            pltpu.VMEM((2 * T, W), BF),
            pltpu.SemaphoreType.DMA((sems,)),
            pltpu.SemaphoreType.DMA((sems,)),
            pltpu.SemaphoreType.DMA((11,)),
        ],
        compiler_params=pltpu.CompilerParams(
            collective_id=0, has_side_effects=True, vmem_limit_bytes=62 * 1024 * 1024),
        cost_estimate=pl.CostEstimate(flops=3_400_000_000, bytes_accessed=40_000_000, transcendentals=0),
    )(q, k, v, wt, dp, *xrefs)


class Scatter:
    def __init__(self, links, source, buf, far, near, far2, near2, final, a, b, load_sem):
        self.L, self.source, self.buf = links, source, buf
        self.farr, self.nearr, self.far2, self.near2, self.final = far, near, far2, near2, final
        self.a, self.b = a, b
        self.rows = final.shape[0]
        self.nb = [[links.number() for _ in range(4)] for _ in range(4)]
        self.na = [links.number() for _ in range(4)]
        self.load = pltpu.make_async_copy(source, buf, load_sem)
        self.load.start()

    def where(self, da, db, half=None):
        L = self.L
        move = {self.a: da, self.b: db}
        x, z = (L.x + move["x"]) % RING, (L.z + move["z"]) % RING
        start, count = 0, self.rows
        if half is not None:
            count = self.rows // 2
            start = half * count
        return pl.ds(pl.multiple_of((x * RING + z) * self.rows + start, 16), count)

    def half(self, h):
        return pl.ds(h * (self.rows // 2), self.rows // 2)

    def begin(self, i):
        da = (2, 3, 1, 0)[i]
        for h, step in ((0, 1), (1, 3)):
            self.L.send(self.nb[i][h], self.source.at[self.where(da, 2, h), :], self.farr.at[i, h], self.b, step)

    def loaded(self):
        self.load.wait()

    def pass_on(self, i):
        da = (2, 3, 1, 0)[i]
        for h, step in ((0, 1), (1, 3)):
            self.L.arrived(self.nb[i][h], self.farr.at[i, h])
            at = self.where(da, step, h)
            self.buf[at, :] = (self.buf[at, :].astype(F32) + self.farr[i, h].astype(F32)).astype(BF)
            self.L.send(self.nb[i][2 + h], self.buf.at[self.where(da, step), :], self.nearr.at[i, h], self.b, step)

    def total(self, i, da, h):
        at = self.where(da, 0, h)
        part = self.half(h)
        return (self.buf[at, :].astype(F32) + self.nearr[i, 0, part, :].astype(F32)
                + self.nearr[i, 1, part, :].astype(F32))

    def close(self, i):
        da = (2, 3, 1, 0)[i]
        for h in range(2):
            self.L.arrived(self.nb[i][2 + h], self.nearr.at[i, h])
        if i == 0:
            for h, step in ((0, 1), (1, 3)):
                at = self.where(da, 0, h)
                self.buf[at, :] = self.total(i, da, h).astype(BF)
                self.L.send(self.na[h], self.buf.at[at, :], self.far2.at[h], self.a, step)
        elif i < 3:
            take = 1 if da == 3 else 0
            self.L.arrived(self.na[take], self.far2.at[take])
            for h in range(2):
                value = self.total(i, da, h)
                if h == take:
                    value += self.far2[take].astype(F32)
                self.buf[self.where(da, 0, h), :] = value.astype(BF)
            self.L.send(self.na[2 + take], self.buf.at[self.where(da, 0), :], self.near2.at[take], self.a, da)

    def finish(self):
        for take in range(2):
            self.L.arrived(self.na[2 + take], self.near2.at[take])
        for h in range(2):
            part = self.half(h)
            value = (self.total(3, 0, h) + self.near2[0, part, :].astype(F32)
                     + self.near2[1, part, :].astype(F32))
            self.final[part, :] = jnp.concatenate(
                [value[i:i + BLK].T for i in range(0, value.shape[0], BLK)], axis=0).astype(BF)


def scatter_kernel(dk, dv, attn, wall, dq, proj, dqo, dko, dvo,
                   bufk, bufv, farr, nearr, far2, near2, final, there, here, halves, wholes, result,
                   send_sems, recv_sems, own_sems):
    L = Links(send_sems, recv_sems)
    other = 1 - L.c
    T = proj.shape[0]
    D = proj.shape[1]
    W = dq.shape[1]
    HD = dk.shape[1]
    L.barrier()
    sk = Scatter(L, dk, bufk, farr.at[0], nearr.at[0], far2.at[0], near2.at[0], final.at[0], "x", "z", own_sems.at[0])
    sv = Scatter(L, dv, bufv, farr.at[1], nearr.at[1], far2.at[1], near2.at[1], final.at[1], "z", "x", own_sems.at[1])
    for i in range(2):
        sk.begin(i)
        sv.begin(i)

    def rows_of(core):
        return pl.ds(pl.multiple_of(core * T, 16), T)

    def heads(ref, core, width):
        return ref.at[:, pl.ds(pl.multiple_of(core * width, 128), width)]

    n_q = L.number()
    L.send(n_q, dq.at[rows_of(other), :], heads(dqo, L.c, W), "c", 1)
    own_q = pltpu.make_async_copy(dq.at[rows_of(L.c), :], heads(dqo, L.c, W), own_sems.at[2])
    own_q.start()

    n_there = [L.number() for _ in range(4)]
    ny = [L.number() for _ in range(4)]
    order = (2, 1, 3, 0)

    def product(core, dy):
        y = (L.y + dy) % RING
        w = wall[pl.ds(pl.multiple_of(y * D, 16), D), :]
        return lax.dot_general(attn[rows_of(core), :], w, (((1,), (1,)), ((), ())), preferred_element_type=F32)

    def away(i):
        here[i] = product(other, order[i]).astype(BF)
        L.send(n_there[i], here.at[i], there.at[i], "c", 1)

    def mine(i):
        value = product(L.c, order[i])
        L.arrived(n_there[i], there.at[i])
        return value + there[i].astype(F32)

    mid = T // 2
    away(0)
    sk.loaded()
    sv.loaded()
    sk.pass_on(0)
    sv.pass_on(0)
    sk.begin(2)
    sv.begin(2)
    away(1)
    sk.pass_on(1)
    sv.pass_on(1)
    sk.begin(3)
    sv.begin(3)
    away(2)
    sk.close(0)
    sv.close(0)
    away(3)
    sk.pass_on(2)
    sv.pass_on(2)
    result[0] = mine(0).astype(BF)
    L.send(ny[0], result.at[0, pl.ds(0, mid), :], halves.at[0], "y", 1)
    L.send(ny[1], result.at[0, pl.ds(mid, mid), :], halves.at[1], "y", 3)
    sk.close(1)
    sv.close(1)
    sk.pass_on(3)
    sv.pass_on(3)
    value = mine(1)
    L.arrived(ny[0], halves.at[0])
    result[1] = jnp.concatenate([value[:mid] + halves[0].astype(F32), value[mid:]], axis=0).astype(BF)
    L.send(ny[2], result.at[1], wholes.at[0], "y", 1)
    value = mine(2)
    L.arrived(ny[1], halves.at[1])
    result[2] = jnp.concatenate([value[:mid], value[mid:] + halves[1].astype(F32)], axis=0).astype(BF)
    L.send(ny[3], result.at[2], wholes.at[1], "y", 3)
    sk.close(2)
    sv.close(2)
    value = mine(3)
    L.arrived(ny[2], wholes.at[0])
    L.arrived(ny[3], wholes.at[1])
    result[3] = (value + wholes[0].astype(F32) + wholes[1].astype(F32)).astype(BF)
    own_p = pltpu.make_async_copy(result.at[3], proj, own_sems.at[3])
    own_p.start()
    outs = []
    for j, (s, out) in enumerate(((sk, dko), (sv, dvo))):
        s.close(3)
        s.finish()
        n = L.number()
        L.send(n, final.at[j, rows_of(other), :], heads(out, L.c, HD), "c", 1)
        own = pltpu.make_async_copy(final.at[j, rows_of(L.c), :], heads(out, L.c, HD), own_sems.at[4 + j])
        own.start()
        outs.append((n, out, own))
    L.arrived(n_q, heads(dqo, other, W))
    own_q.wait()
    own_p.wait()
    for n, out, own in outs:
        L.arrived(n, heads(out, other, HD))
        own.wait()
    L.finish()


def scatter(dk, dv, attn, wall, dq, D):
    T = dq.shape[0] // 2
    W = dq.shape[1]
    HD = dk.shape[1]
    anywhere = pl.BlockSpec(memory_space=pltpu.HBM)
    vmem = pl.BlockSpec(memory_space=pltpu.VMEM)
    sems = 64
    return pl.pallas_call(
        scatter_kernel,
        out_shape=(
            jax.ShapeDtypeStruct((T, D), BF),
            jax.ShapeDtypeStruct((T, 2 * W), BF),
            jax.ShapeDtypeStruct((T, 2 * HD), BF),
            jax.ShapeDtypeStruct((T, 2 * HD), BF),
        ),
        in_specs=[anywhere, anywhere, vmem, vmem, anywhere],
        out_specs=(anywhere,) * 4,
        scratch_shapes=[
            pltpu.VMEM(dk.shape, BF),
            pltpu.VMEM(dk.shape, BF),
            pltpu.VMEM((2, 4, 2, T, HD), BF),
            pltpu.VMEM((2, 4, 2, 2 * T, HD), BF),
            pltpu.VMEM((2, 2, T, HD), BF),
            pltpu.VMEM((2, 2, 2 * T, HD), BF),
            pltpu.VMEM((2, 2 * T, HD), BF),
            pltpu.VMEM((4, T, D), BF),
            pltpu.VMEM((4, T, D), BF),
            pltpu.VMEM((2, T // 2, D), BF),
            pltpu.VMEM((2, T, D), BF),
            pltpu.VMEM((4, T, D), BF),
            pltpu.SemaphoreType.DMA((sems,)),
            pltpu.SemaphoreType.DMA((sems,)),
            pltpu.SemaphoreType.DMA((6,)),
        ],
        compiler_params=pltpu.CompilerParams(
            collective_id=1, has_side_effects=True, vmem_limit_bytes=62 * 1024 * 1024),
        cost_estimate=pl.CostEstimate(flops=3_400_000_000, bytes_accessed=40_000_000, transcendentals=0),
    )(dk, dv, attn, wall, dq)


def hand_on_kernel(*refs):
    count = (len(refs) - 1) // 2
    sems = refs[-1]
    copies = []
    for src, dst in zip(refs[:count], refs[count:-1]):
        rows = src.shape[0] // 4
        for i in range(4):
            part = pl.ds(i * rows, rows)
            copies.append(pltpu.make_async_copy(src.at[part, :], dst.at[part, :], sems.at[len(copies)]))
            copies[-1].start()
    for copy in copies:
        copy.wait()


def hand_on(*arrays):
    hbm = pl.BlockSpec(memory_space=pltpu.HBM)
    return pl.pallas_call(
        hand_on_kernel,
        out_shape=tuple(jax.ShapeDtypeStruct(a.shape, a.dtype) for a in arrays),
        in_specs=[hbm] * len(arrays),
        out_specs=(hbm,) * len(arrays),
        scratch_shapes=[pltpu.SemaphoreType.DMA((4 * len(arrays),))],
        compiler_params=pltpu.CompilerParams(vmem_limit_bytes=62 * 1024 * 1024),
        cost_estimate=pl.CostEstimate(flops=0, bytes_accessed=5_000_000, transcendentals=0),
    )(*arrays)


def on_device(queries, keys, values, out_weight, d_proj, block_section, section_parent, xref_owner, xref_block, xref_valid):
    seq = lax.axis_size("seq")
    qh, kall, vall, wall, d_attn, *xrefs = gather(
        queries, keys, values, out_weight.T, d_proj, (xref_owner, xref_block, xref_valid), seq)
    attn, dq, dk, dv = attention(block_section, section_parent, xrefs, qh, kall, vall, d_attn)
    return hand_on(*scatter(dk, dv, attn, wall, dq, d_proj.shape[1]))


def solution(mesh):
    split = P("seq", "head")
    rows = P("seq", None)
    return jax.shard_map(
        on_device, mesh=mesh,
        in_specs=(split, split, split, P("head", "seq"), split, P(), P(), rows, rows, rows),
        out_specs=(split,) * 4, check_vma=False)
```

```python
import functools
import jax, jax.numpy as jnp
from jax import lax
from jax.experimental import pallas as pl
from jax.experimental.pallas import tpu as pltpu
from jax.sharding import PartitionSpec as P
F32, BF = jnp.float32, jnp.bfloat16
MESH = pl.DeviceIdType.MESH
RING = 4


HD = 128
BLK = 128
CHUNK = 4
BOTH = 2


def attention_kernel(NBLK, NSEC, NQ, G, XR, sec_hbm, par_hbm, xo_hbm, xb_hbm, xv_hbm, q_hbm, k_hbm, v_hbm, do_hbm, attn_hbm, dq_hbm, dk_hbm, dv_hbm,
                     kc, vc, ak, av, sbuf0, sbuf1, q_ref, do_ref, attn_ref, dq_ref, dk_ref, dv_ref,
                     qs_t, dot_t, ot0, ot1, shares, slots, counts, first, stop, done, sec, parent, xo, xb, xv, sems):
    scaling = HD ** -0.5
    sbuf, ot = (sbuf0, sbuf1), (ot0, ot1)
    NT = (((1,), (1,)), ((), ()))
    TN = (((0,), (0,)), ((), ()))
    NN = (((1,), (0,)), ((), ()))
    R = CHUNK * BLK

    def mm(a, b, dims):
        return lax.dot_general(a, b, dims, preferred_element_type=F32)

    loads = [pltpu.make_async_copy(src, dst, sems.at[i]) for i, (src, dst) in enumerate((
        (k_hbm, kc.at[pl.ds(0, NBLK * BLK)]), (v_hbm, vc.at[pl.ds(0, NBLK * BLK)]), (q_hbm, q_ref), (do_hbm, do_ref)))]
    tables = [pltpu.make_async_copy(src, dst, sems.at[16 + i]) for i, (src, dst) in enumerate((
        (sec_hbm, sec), (par_hbm, parent), (xo_hbm, xo), (xb_hbm, xb), (xv_hbm, xv)))]
    for copy in tables + loads:
        copy.start()
    for copy in tables:
        copy.wait()
    begin = (lax.axis_index("seq") // 2) * NQ

    @pl.loop(0, NSEC)
    def _(s):
        stop[s] = 0
        first[s] = 0
        done[s] = 0

    @pl.loop(0, NBLK // 8)
    def _(i):
        for h in range(8):
            c = i * 8 + h
            stop[sec[c]] = c + 1
            d = NBLK - 1 - c
            first[sec[d]] = d

    @pl.loop(0, NQ)
    def _(b):
        g = begin + b
        mine = sec[g]
        for j in range(32):
            slots[b, j] = g
        slots[b, 1] = NBLK + mine
        n = jnp.int32(2)
        for w in (1, 2, 3):
            c = g - w
            cs = jnp.maximum(c, 0)
            slots[b, n] = cs
            n = n + jnp.where((c >= 0) & (sec[cs] == mine), 1, 0)
        up = parent[mine]
        slots[b, n] = NBLK + jnp.maximum(up, 0)
        n = n + jnp.where(up >= 0, 1, 0)
        core, row = lax.div(b, NQ // 2), lax.rem(b, NQ // 2)
        for j in range(XR):
            slots[b, n] = xo[core, row * XR + j, 0] * (NQ // 2) + xb[core, row, j] + 256
            n = n + jnp.where(xv[core, row, j] > 0, 1, 0)
        slots[b, n] = g
        counts[b] = n

    @pl.loop(0, (NBLK + NSEC) // 4)
    def _(i):
        at = pl.ds(pl.multiple_of(i * 512, 512), 512)
        ak[at, :] = jnp.zeros((512, HD), F32)
        av[at, :] = jnp.zeros((512, HD), F32)

    for copy in loads:
        copy.wait()

    def span(i):
        return pl.ds(pl.multiple_of(i * BLK, BLK), BLK)

    def summarize(s):
        def add(c, t):
            return t[0] + kc[span(c), :].astype(F32), t[1] + vc[span(c), :].astype(F32)
        zero = jnp.zeros((BLK, HD), F32)
        tk, tv = lax.fori_loop(first[s], stop[s], add, (zero, zero))
        share = 1.0 / jnp.sqrt(jnp.full((8, HD), jnp.maximum(stop[s] - first[s], 1)).astype(F32))
        shares[s] = share
        kc[span(NBLK + s), :] = (tk * share[:1]).astype(BF)
        vc[span(NBLK + s), :] = (tv * share[:1]).astype(BF)
        done[s] = 1

    @pl.loop(0, 2 * NQ)
    def _(i):
        mine = sec[begin + lax.div(i, 2)]
        s = jnp.where(lax.rem(i, 2) == 0, mine, jnp.maximum(parent[mine], 0))

        @pl.when(done[s] == 0)
        def _():
            summarize(s)

    W = G * BLK
    row_id = lax.broadcasted_iota(jnp.int32, (BLK, BLK), 0)
    col_id = lax.broadcasted_iota(jnp.int32, (BLK, BLK), 1)
    causal = jnp.concatenate([row_id <= col_id] * G, axis=1)

    def fold(op, s):
        return op(s.reshape(s.shape[0] // 8, 8, W), axis=0)

    ones = jnp.ones((R, 16), BF)

    TWO = range(BOTH)

    @pl.loop(0, NQ // BOTH)
    def _(u):
        bs = [u * BOTH + t for t in TWO]
        bases = [pl.multiple_of(b * BLK, BLK) for b in bs]
        for t in TWO:
            for g in range(G):
                part = slice(g * BLK, (g + 1) * BLK)
                qs_t[t, :, part] = q_ref[pl.ds(bases[t], BLK), part].astype(F32).T.astype(BF)
                dot_t[t, :, part] = do_ref[pl.ds(bases[t], BLK), part].astype(F32).T.astype(BF)
        ns = [counts[b] for b in bs]
        most = ns[0]
        for n in ns[1:]:
            most = jnp.maximum(most, n)
        chunks = lax.div(most + CHUNK - 1, CHUNK)

        def chunk(t, ref, j):
            return jnp.concatenate([ref[span(slots[bs[t], CHUNK * j + h] & 255), :] for h in range(CHUNK)], axis=0)

        def rows(j):
            return pl.ds(pl.multiple_of(j * R, R), R)

        def scores(t, j):
            s = mm(chunk(t, kc, j), qs_t[t], NN) * scaling
            return jnp.concatenate([
                s[h * BLK:(h + 1) * BLK] + jnp.where(CHUNK * j + h < ns[t], 0.0, -1e30) for h in range(CHUNK)], axis=0)

        tops = []
        for t in TWO:
            s0 = scores(t, 0)
            s0 = jnp.concatenate([jnp.where(causal, s0[:BLK], -1e30), s0[BLK:]], axis=0)
            sbuf[t][rows(0), :] = s0
            tops.append(fold(jnp.max, s0))

        def score(j, ms):
            ss = [scores(t, j) for t in TWO]
            for t in TWO:
                sbuf[t][rows(j), :] = ss[t]
            return tuple(jnp.maximum(ms[t], fold(jnp.max, ss[t])) for t in TWO)
        tops = lax.fori_loop(1, chunks, score, tuple(tops))
        tops = [jnp.max(m, axis=0, keepdims=True) for m in tops]

        for t in TWO:
            ot[t][...] = jnp.zeros((HD + 16, W), F32)

        def forward(j, carry):
            es = [jnp.exp(sbuf[t][rows(j), :] - tops[t]) for t in TWO]
            for t in TWO:
                sbuf[t][rows(j), :] = es[t]
            for t in TWO:
                ot[t][...] += mm(jnp.concatenate([chunk(t, vc, j), ones], axis=1), es[t].astype(BF), TN)
            return carry
        lax.fori_loop(0, chunks, forward, 0)
        rls, deltas = [], []
        for t in TWO:
            rl = 1.0 / ot[t][HD:HD + 1, :]
            o_t = (ot[t][:HD, :] * rl).astype(BF).astype(F32)
            rls.append(rl)
            deltas.append(jnp.sum(o_t * dot_t[t].astype(F32), axis=0, keepdims=True))
            for g in range(G):
                part = slice(g * BLK, (g + 1) * BLK)
                attn_ref[pl.ds(bases[t], BLK), part] = o_t[:, part].T.astype(BF)

        def put(acc, t, i, term):
            slot = slots[bs[t], i]
            where = span(slot & 255)
            acc[where, :] += jnp.where(slot >= 256, term.astype(BF).astype(F32), term)

        for t in TWO:
            ot[t][:HD, :] = jnp.zeros((HD, W), F32)

        def backward(j, carry):
            terms = []
            for t in TWO:
                k, v = chunk(t, kc, j), chunk(t, vc, j)
                p = sbuf[t][rows(j), :] * rls[t]
                ds = (p * (mm(v, dot_t[t], NN) - deltas[t])).astype(BF)
                dv = mm(dot_t[t], p.astype(BF), NT)
                dk = mm(qs_t[t], ds, NT) * scaling
                ot[t][:HD, :] += mm(k, ds, TN)
                terms.append((dk, dv))
            for t in TWO:
                dk, dv = terms[t]
                for h in range(CHUNK):
                    put(ak, t, CHUNK * j + h, dk[:, h * BLK:(h + 1) * BLK])
                    put(av, t, CHUNK * j + h, dv[:, h * BLK:(h + 1) * BLK])
            return carry
        lax.fori_loop(0, chunks, backward, 0)
        for t in TWO:
            for g in range(G):
                part = slice(g * BLK, (g + 1) * BLK)
                dq_ref[pl.ds(bases[t], BLK), part] = (ot[t][:HD, part] * scaling).T.astype(BF)

    saves = [pltpu.make_async_copy(attn_ref, attn_hbm, sems.at[4]), pltpu.make_async_copy(dq_ref, dq_hbm, sems.at[5])]
    for copy in saves:
        copy.start()
    @pl.loop(0, NSEC)
    def _(s):
        @pl.when(done[s] == 1)
        def _():
            share = shares[s][:1]
            gk, gv = ak[span(NBLK + s), :] * share, av[span(NBLK + s), :] * share

            @pl.loop(first[s], stop[s])
            def _(c):
                ak[span(c), :] += gk
                av[span(c), :] += gv

    STEP = 4
    PARTS = 4

    for part in range(PARTS):
        size = NBLK // PARTS

        @pl.loop(part * size // STEP, (part + 1) * size // STEP)
        def _(i):
            at = pl.ds(pl.multiple_of(i * STEP * BLK, STEP * BLK), STEP * BLK)
            dk_ref[at, :] = ak[at, :].astype(BF)
            dv_ref[at, :] = av[at, :].astype(BF)
        at = pl.ds(part * size * BLK, size * BLK)
        for j, (src, dst) in enumerate(((dk_ref, dk_hbm), (dv_ref, dv_hbm))):
            copy = pltpu.make_async_copy(src.at[at, :], dst.at[at, :], sems.at[6 + 2 * part + j])
            copy.start()
            saves.append(copy)
    for copy in saves:
        copy.wait()


def attention(block_section, section_parent, xrefs, q, k, v, do):
    NSEC = section_parent.shape[0]
    XR = xrefs[1].shape[2]
    NBLK = k.shape[0] // BLK
    NQ = q.shape[0] // BLK
    G = q.shape[1] // HD
    W = G * BLK
    slots_most = -(-(6 + XR) // CHUNK) * CHUNK
    hbm = pl.BlockSpec(memory_space=pltpu.HBM)
    every = ((NBLK + NSEC) * BLK, HD)
    return pl.pallas_call(
        functools.partial(attention_kernel, NBLK, NSEC, NQ, G, XR),
        out_shape=(jax.ShapeDtypeStruct(q.shape, BF), jax.ShapeDtypeStruct(q.shape, BF),
                   jax.ShapeDtypeStruct(k.shape, BF), jax.ShapeDtypeStruct(k.shape, BF)),
        in_specs=[hbm] * 9,
        out_specs=(hbm,) * 4,
        scratch_shapes=[
            pltpu.VMEM(every, BF),
            pltpu.VMEM(every, BF),
            pltpu.VMEM(every, F32),
            pltpu.VMEM(every, F32),
            pltpu.VMEM((slots_most * BLK, W), F32),
            pltpu.VMEM((slots_most * BLK, W), F32),
            pltpu.VMEM(q.shape, BF),
            pltpu.VMEM(q.shape, BF),
            pltpu.VMEM(q.shape, BF),
            pltpu.VMEM(q.shape, BF),
            pltpu.VMEM(k.shape, BF),
            pltpu.VMEM(k.shape, BF),
            pltpu.VMEM((BOTH, HD, W), BF),
            pltpu.VMEM((BOTH, HD, W), BF),
            pltpu.VMEM((HD + 16, W), F32),
            pltpu.VMEM((HD + 16, W), F32),
            pltpu.VMEM((NSEC, 8, HD), F32),
            pltpu.SMEM((NQ, 32), jnp.int32),
            pltpu.SMEM((NQ,), jnp.int32),
            pltpu.SMEM((NSEC,), jnp.int32),
            pltpu.SMEM((NSEC,), jnp.int32),
            pltpu.SMEM((NSEC,), jnp.int32),
            pltpu.SMEM(block_section.shape, jnp.int32),
            pltpu.SMEM(section_parent.shape, jnp.int32),
        ] + [pltpu.SMEM(a.shape, jnp.int32) for a in xrefs] + [
            pltpu.SemaphoreType.DMA((24,)),
        ],
        compiler_params=pltpu.CompilerParams(vmem_limit_bytes=62 * 1024 * 1024),
        cost_estimate=pl.CostEstimate(flops=18_000_000_000, bytes_accessed=24_000_000, transcendentals=12_000_000),
    )(block_section, section_parent, *xrefs, q, k, v, do)


class Links:
    def __init__(self, send_sems, recv_sems):
        s = lax.axis_index("seq")
        self.y = lax.axis_index("head")
        self.x = s // 8
        self.z = (s // 2) % RING
        self.c = s % 2
        self.send_sems, self.recv_sems = send_sems, recv_sems
        self.used = 0
        self.sent = []

    def device(self, axis, step):
        x, z, y, c = self.x, self.z, self.y, self.c
        if axis == "x":
            x = (x + step) % RING
        elif axis == "z":
            z = (z + step) % RING
        elif axis == "y":
            y = (y + step) % RING
        else:
            c = 1 - c
        return ((x * RING + z) * 2 + c, y)

    def everyone(self):
        return [self.device(a, d) for a in "xzy" for d in (1, RING - 1)] + [self.device("c", 1)]

    def barrier(self):
        sem = pltpu.get_barrier_semaphore()
        for device in self.everyone():
            pl.semaphore_signal(sem, inc=1, device_id=device, device_id_type=MESH)
        pl.semaphore_wait(sem, 7)

    def number(self):
        self.used += 1
        return self.used - 1

    def send(self, number, src, dst, axis, step):
        copy = pltpu.make_async_remote_copy(
            src_ref=src, dst_ref=dst, send_sem=self.send_sems.at[number], recv_sem=self.recv_sems.at[number],
            device_id=self.device(axis, step), device_id_type=MESH)
        copy.start()
        self.sent.append(copy)

    def arrived(self, number, dst):
        pltpu.make_async_remote_copy(
            src_ref=dst, dst_ref=dst, send_sem=self.send_sems.at[number], recv_sem=self.recv_sems.at[number],
            device_id=self.device("c", 1), device_id_type=MESH).wait_recv()

    def finish(self):
        for copy in self.sent:
            copy.wait_send()


class Gather:
    def __init__(self, links, array, rows, pitch, offset, split, a, b):
        self.L, self.array, self.rows, self.pitch, self.offset, self.split = links, array, rows, pitch, offset, split
        self.a, self.b = a, b
        self.na = [links.number() for _ in range(4)]
        self.nb = [[links.number() for _ in range(4)] for _ in range(4)]

    def at(self, da, db, half=None):
        L = self.L
        move = {self.a: da, self.b: db}
        x, z = (L.x + move["x"]) % RING, (L.z + move["z"]) % RING
        start, count = self.offset, self.rows
        if half == 0:
            count = self.split
        elif half == 1:
            start, count = self.offset + self.split, self.rows - self.split
        return self.array.at[pl.ds(pl.multiple_of((x * RING + z) * self.pitch + start, 16), count), :]

    def put(self, number, axis, step, da, db, half=None):
        self.L.send(number, self.at(da, db, half), self.at(da, db, half), axis, step)

    def begin(self):
        self.put(self.na[0], self.a, 1, 0, 0)
        self.put(self.na[1], self.a, 3, 0, 0)

    def spread(self, i, da):
        self.put(self.nb[i][0], self.b, 1, da, 0)
        self.put(self.nb[i][1], self.b, 3, da, 0)

    def near(self):
        self.L.arrived(self.na[0], self.at(3, 0))
        self.put(self.na[2], self.a, 1, 3, 0, 0)
        self.L.arrived(self.na[1], self.at(1, 0))
        self.put(self.na[3], self.a, 3, 1, 0, 1)
        self.spread(0, 0)
        self.spread(1, 3)
        self.spread(2, 1)

    def far(self):
        self.L.arrived(self.na[2], self.at(2, 0, 0))
        self.L.arrived(self.na[3], self.at(2, 0, 1))
        self.spread(3, 2)

    def relay(self, i):
        da = (0, 3, 1, 2)[i]
        self.L.arrived(self.nb[i][0], self.at(da, 3))
        self.put(self.nb[i][2], self.b, 1, da, 3, 0)
        self.L.arrived(self.nb[i][1], self.at(da, 1))
        self.put(self.nb[i][3], self.b, 3, da, 1, 1)

    def end(self, i):
        da = (0, 3, 1, 2)[i]
        self.L.arrived(self.nb[i][2], self.at(da, 2, 0))
        self.L.arrived(self.nb[i][3], self.at(da, 2, 1))


def gather_kernel(q_hbm, k_hbm, v_hbm, wt_hbm, dp_hbm, xo, xb, xv, qh, kall, vall, wall, dattn, xos, xbs, xvs, q, k, v, wt, dp, wbuf, dbuf, abuf, send_sems, recv_sems, own_sems):
    L = Links(send_sems, recv_sems)
    chip = L.x * RING + L.z
    other = 1 - L.c
    T = k.shape[0]
    HD = kall.shape[1]
    W = qh.shape[1]
    C = wt.shape[0]
    D = dp.shape[1]
    loads = [pltpu.make_async_copy(src, dst, own_sems.at[11 + i]) for i, (src, dst) in enumerate((
        (wt_hbm, wt), (k_hbm, k), (v_hbm, v), (dp_hbm, dp), (q_hbm, q)))]
    for copy in loads:
        copy.start()
    L.barrier()
    for copy in loads:
        copy.wait()

    pairs = []

    def split(src, width, dst, first, rows):
        at = dst.at[pl.ds(pl.multiple_of(first, 16), rows), :]
        pairs.append((L.number(), src, width, dst, at, rows))

    mine = chip * 2 * T + L.c * T
    split(wt, W, wbuf, chip * 2 * C + L.c * C, C)
    split(k, HD, kall, mine, T)
    split(v, HD, vall, mine, T)
    split(q, W, qh, L.c * T, T)
    own = []
    for i, (number, src, width, dst, at, rows) in enumerate(pairs):
        L.send(number, src.at[:, pl.ds(pl.multiple_of(other * width, 128), width)], at, "c", 1)
        copy = pltpu.make_async_copy(src.at[:, pl.ds(pl.multiple_of(L.c * width, 128), width)], at, own_sems.at[i])
        copy.start()
        own.append(copy)
    refs = []
    for i, (src, dst) in enumerate(((xo, xos), (xb, xbs), (xv, xvs))):
        n = L.number()
        L.send(n, src, dst.at[L.c], "c", 1)
        copy = pltpu.make_async_copy(src, dst.at[L.c], own_sems.at[8 + i])
        copy.start()
        refs.append((n, dst, copy))

    def piece(core, dy, half=None):
        ref = dbuf.at[core * RING + (L.y + dy) % RING]
        if half is None:
            return ref
        return ref.at[pl.ds(half * (T // 2), T // 2), :]

    ny = [L.number() for _ in range(4)]
    nc = [L.number() for _ in range(4)]
    L.send(ny[0], dp, piece(L.c, 0), "y", 1)
    L.send(ny[1], dp, piece(L.c, 0), "y", 3)
    L.send(nc[0], dp, piece(L.c, 0), "c", 1)
    own_d = pltpu.make_async_copy(dp, piece(L.c, 0), own_sems.at[5])
    own_d.start()

    sibling = [chip * 2 * C + other * C, chip * 2 * T + other * T, chip * 2 * T + other * T, other * T]

    def both(i):
        number, src, width, dst, at, rows = pairs[i]
        L.arrived(number, dst.at[pl.ds(pl.multiple_of(sibling[i], 16), rows), :])
        own[i].wait()

    first_w = (C // 2 + 15) // 16 * 16
    w0 = Gather(L, wbuf, C, 2 * C, 0, first_w, "x", "z")
    w1 = Gather(L, wbuf, C, 2 * C, C, first_w, "z", "x")
    gk = Gather(L, kall, 2 * T, 2 * T, 0, T, "x", "z")
    gv = Gather(L, vall, 2 * T, 2 * T, 0, T, "z", "x")
    both(0)
    w0.begin()
    w1.begin()
    both(1)
    gk.begin()
    both(2)
    gv.begin()
    w0.near()
    w1.near()
    gk.near()
    gv.near()
    w0.far()
    w1.far()
    gk.far()
    gv.far()
    L.arrived(ny[0], piece(L.c, 3))
    L.send(ny[2], piece(L.c, 3, 0), piece(L.c, 3, 0), "y", 1)
    L.arrived(ny[1], piece(L.c, 1))
    L.send(ny[3], piece(L.c, 1, 1), piece(L.c, 1, 1), "y", 3)
    L.send(nc[1], piece(L.c, 3), piece(L.c, 3), "c", 1)
    L.send(nc[2], piece(L.c, 1), piece(L.c, 1), "c", 1)
    for i in range(4):
        w0.relay(i)
        w1.relay(i)
    for i in range(2):
        gk.relay(i)
        gv.relay(i)
    L.arrived(ny[2], piece(L.c, 2, 0))
    L.arrived(ny[3], piece(L.c, 2, 1))
    L.send(nc[3], piece(L.c, 2), piece(L.c, 2), "c", 1)
    for i in range(4):
        w0.end(i)
        w1.end(i)
    keep = pltpu.make_async_copy(wbuf, wall, own_sems.at[6])
    keep.start()

    step = 256

    def product(core, t):
        rows = pl.ds(pl.multiple_of(t * step, step), step)
        total = jnp.zeros((step, W), F32)
        for y in range(RING):
            total += jnp.dot(dbuf[core * RING + y, rows, :], wbuf[y * D:(y + 1) * D, :], preferred_element_type=F32)
        abuf[pl.ds(pl.multiple_of(core * T + t * step, step), step), :] = total.astype(BF)

    def products(core):
        @pl.loop(0, T // step)
        def _(t):
            product(core, t)

    gk.relay(2)
    gv.relay(2)
    own_d.wait()
    products(L.c)
    gk.relay(3)
    gv.relay(3)
    for i, dy in enumerate((0, 3, 1, 2)):
        L.arrived(nc[i], piece(other, dy))
    products(other)
    save = pltpu.make_async_copy(abuf, dattn, own_sems.at[7])
    save.start()
    for i in range(4):
        gk.end(i)
        gv.end(i)
    both(3)
    for n, dst, copy in refs:
        L.arrived(n, dst.at[other])
        copy.wait()
    keep.wait()
    save.wait()
    L.finish()


def gather(q, k, v, wt, dp, xrefs, seq):
    T = k.shape[0]
    HD = k.shape[1] // 2
    W = q.shape[1] // 2
    C = wt.shape[0]
    D = dp.shape[1]
    anywhere = pl.BlockSpec(memory_space=pltpu.HBM)
    sems = 128
    return pl.pallas_call(
        gather_kernel,
        out_shape=(
            jax.ShapeDtypeStruct((2 * T, W), BF),
            jax.ShapeDtypeStruct((seq * T, HD), BF),
            jax.ShapeDtypeStruct((seq * T, HD), BF),
            jax.ShapeDtypeStruct((seq * C, W), BF),
            jax.ShapeDtypeStruct((2 * T, W), BF),
        ) + tuple(jax.ShapeDtypeStruct((2,) + a.shape, jnp.int32) for a in xrefs),
        in_specs=[anywhere] * 8,
        out_specs=(anywhere,) * 8,
        scratch_shapes=[pltpu.VMEM(a.shape, BF) for a in (q, k, v, wt, dp)] + [
            pltpu.VMEM((seq * C, W), BF),
            pltpu.VMEM((2 * RING, T, D), BF),
            pltpu.VMEM((2 * T, W), BF),
            pltpu.SemaphoreType.DMA((sems,)),
            pltpu.SemaphoreType.DMA((sems,)),
            pltpu.SemaphoreType.DMA((16,)),
        ],
        compiler_params=pltpu.CompilerParams(
            collective_id=0, has_side_effects=True, vmem_limit_bytes=62 * 1024 * 1024),
        cost_estimate=pl.CostEstimate(flops=3_400_000_000, bytes_accessed=40_000_000, transcendentals=0),
    )(q, k, v, wt, dp, *xrefs)


class Scatter:
    def __init__(self, links, source, buf, far, near, far2, near2, final, a, b, load_sem):
        self.L, self.source, self.buf = links, source, buf
        self.farr, self.nearr, self.far2, self.near2, self.final = far, near, far2, near2, final
        self.a, self.b = a, b
        self.rows = final.shape[0]
        self.nb = [[links.number() for _ in range(4)] for _ in range(4)]
        self.na = [links.number() for _ in range(4)]
        self.load = pltpu.make_async_copy(source, buf, load_sem)
        self.load.start()

    def where(self, da, db, half=None):
        L = self.L
        move = {self.a: da, self.b: db}
        x, z = (L.x + move["x"]) % RING, (L.z + move["z"]) % RING
        start, count = 0, self.rows
        if half is not None:
            count = self.rows // 2
            start = half * count
        return pl.ds(pl.multiple_of((x * RING + z) * self.rows + start, 16), count)

    def half(self, h):
        return pl.ds(h * (self.rows // 2), self.rows // 2)

    def begin(self, i):
        da = (2, 3, 1, 0)[i]
        for h, step in ((0, 1), (1, 3)):
            self.L.send(self.nb[i][h], self.source.at[self.where(da, 2, h), :], self.farr.at[i, h], self.b, step)

    def loaded(self):
        self.load.wait()

    def pass_on(self, i):
        da = (2, 3, 1, 0)[i]
        for h, step in ((0, 1), (1, 3)):
            self.L.arrived(self.nb[i][h], self.farr.at[i, h])
            at = self.where(da, step, h)
            self.buf[at, :] = (self.buf[at, :].astype(F32) + self.farr[i, h].astype(F32)).astype(BF)
            self.L.send(self.nb[i][2 + h], self.buf.at[self.where(da, step), :], self.nearr.at[i, h], self.b, step)

    def total(self, i, da, h):
        at = self.where(da, 0, h)
        part = self.half(h)
        return (self.buf[at, :].astype(F32) + self.nearr[i, 0, part, :].astype(F32)
                + self.nearr[i, 1, part, :].astype(F32))

    def close(self, i):
        da = (2, 3, 1, 0)[i]
        for h in range(2):
            self.L.arrived(self.nb[i][2 + h], self.nearr.at[i, h])
        if i == 0:
            for h, step in ((0, 1), (1, 3)):
                at = self.where(da, 0, h)
                self.buf[at, :] = self.total(i, da, h).astype(BF)
                self.L.send(self.na[h], self.buf.at[at, :], self.far2.at[h], self.a, step)
        elif i < 3:
            take = 1 if da == 3 else 0
            self.L.arrived(self.na[take], self.far2.at[take])
            for h in range(2):
                value = self.total(i, da, h)
                if h == take:
                    value += self.far2[take].astype(F32)
                self.buf[self.where(da, 0, h), :] = value.astype(BF)
            self.L.send(self.na[2 + take], self.buf.at[self.where(da, 0), :], self.near2.at[take], self.a, da)

    def finish(self):
        for take in range(2):
            self.L.arrived(self.na[2 + take], self.near2.at[take])
        for h in range(2):
            part = self.half(h)
            value = (self.total(3, 0, h) + self.near2[0, part, :].astype(F32)
                     + self.near2[1, part, :].astype(F32))
            self.final[part, :] = jnp.concatenate(
                [value[i:i + BLK].T for i in range(0, value.shape[0], BLK)], axis=0).astype(BF)


def scatter_kernel(dk, dv, attn, wall, dq_hbm, proj, dqo, dko, dvo,
                   dq, bufk, bufv, farr, nearr, far2, near2, final, there, here, halves, wholes, result,
                   send_sems, recv_sems, own_sems):
    L = Links(send_sems, recv_sems)
    other = 1 - L.c
    T = proj.shape[0]
    D = proj.shape[1]
    W = dq.shape[1]
    HD = dk.shape[1]
    load_q = pltpu.make_async_copy(dq_hbm, dq, own_sems.at[6])
    load_q.start()
    L.barrier()
    sk = Scatter(L, dk, bufk, farr.at[0], nearr.at[0], far2.at[0], near2.at[0], final.at[0], "x", "z", own_sems.at[0])
    sv = Scatter(L, dv, bufv, farr.at[1], nearr.at[1], far2.at[1], near2.at[1], final.at[1], "z", "x", own_sems.at[1])
    for i in range(2):
        sk.begin(i)
        sv.begin(i)

    def rows_of(core):
        return pl.ds(pl.multiple_of(core * T, 16), T)

    def heads(ref, core, width):
        return ref.at[:, pl.ds(pl.multiple_of(core * width, 128), width)]

    load_q.wait()
    n_q = L.number()
    L.send(n_q, dq.at[rows_of(other), :], heads(dqo, L.c, W), "c", 1)
    own_q = pltpu.make_async_copy(dq.at[rows_of(L.c), :], heads(dqo, L.c, W), own_sems.at[2])
    own_q.start()

    n_there = [L.number() for _ in range(4)]
    ny = [L.number() for _ in range(4)]
    order = (2, 1, 3, 0)

    def product(core, dy):
        y = (L.y + dy) % RING
        w = wall[pl.ds(pl.multiple_of(y * D, 16), D), :]
        return lax.dot_general(attn[rows_of(core), :], w, (((1,), (1,)), ((), ())), preferred_element_type=F32)

    def away(i):
        here[i] = product(other, order[i]).astype(BF)
        L.send(n_there[i], here.at[i], there.at[i], "c", 1)

    def mine(i):
        value = product(L.c, order[i])
        L.arrived(n_there[i], there.at[i])
        return value + there[i].astype(F32)

    mid = T // 2
    away(0)
    sk.loaded()
    sv.loaded()
    sk.pass_on(0)
    sv.pass_on(0)
    sk.begin(2)
    sv.begin(2)
    away(1)
    sk.pass_on(1)
    sv.pass_on(1)
    sk.begin(3)
    sv.begin(3)
    away(2)
    sk.close(0)
    sv.close(0)
    away(3)
    sk.pass_on(2)
    sv.pass_on(2)
    result[0] = mine(0).astype(BF)
    L.send(ny[0], result.at[0, pl.ds(0, mid), :], halves.at[0], "y", 1)
    L.send(ny[1], result.at[0, pl.ds(mid, mid), :], halves.at[1], "y", 3)
    sk.close(1)
    sv.close(1)
    sk.pass_on(3)
    sv.pass_on(3)
    value = mine(1)
    L.arrived(ny[0], halves.at[0])
    result[1] = jnp.concatenate([value[:mid] + halves[0].astype(F32), value[mid:]], axis=0).astype(BF)
    L.send(ny[2], result.at[1], wholes.at[0], "y", 1)
    value = mine(2)
    L.arrived(ny[1], halves.at[1])
    result[2] = jnp.concatenate([value[:mid], value[mid:] + halves[1].astype(F32)], axis=0).astype(BF)
    L.send(ny[3], result.at[2], wholes.at[1], "y", 3)
    sk.close(2)
    sv.close(2)
    value = mine(3)
    L.arrived(ny[2], wholes.at[0])
    L.arrived(ny[3], wholes.at[1])
    result[3] = (value + wholes[0].astype(F32) + wholes[1].astype(F32)).astype(BF)
    own_p = pltpu.make_async_copy(result.at[3], proj, own_sems.at[3])
    own_p.start()
    outs = []
    for j, (s, out) in enumerate(((sk, dko), (sv, dvo))):
        s.close(3)
        s.finish()
        n = L.number()
        L.send(n, final.at[j, rows_of(other), :], heads(out, L.c, HD), "c", 1)
        own = pltpu.make_async_copy(final.at[j, rows_of(L.c), :], heads(out, L.c, HD), own_sems.at[4 + j])
        own.start()
        outs.append((n, out, own))
    L.arrived(n_q, heads(dqo, other, W))
    own_q.wait()
    own_p.wait()
    for n, out, own in outs:
        L.arrived(n, heads(out, other, HD))
        own.wait()
    L.finish()


def scatter(dk, dv, attn, wall, dq, D):
    T = dq.shape[0] // 2
    W = dq.shape[1]
    HD = dk.shape[1]
    anywhere = pl.BlockSpec(memory_space=pltpu.HBM)
    vmem = pl.BlockSpec(memory_space=pltpu.VMEM)
    sems = 64
    return pl.pallas_call(
        scatter_kernel,
        out_shape=(
            jax.ShapeDtypeStruct((T, D), BF),
            jax.ShapeDtypeStruct((T, 2 * W), BF),
            jax.ShapeDtypeStruct((T, 2 * HD), BF),
            jax.ShapeDtypeStruct((T, 2 * HD), BF),
        ),
        in_specs=[anywhere, anywhere, vmem, vmem, anywhere],
        out_specs=(anywhere,) * 4,
        scratch_shapes=[
            pltpu.VMEM(dq.shape, BF),
            pltpu.VMEM(dk.shape, BF),
            pltpu.VMEM(dk.shape, BF),
            pltpu.VMEM((2, 4, 2, T, HD), BF),
            pltpu.VMEM((2, 4, 2, 2 * T, HD), BF),
            pltpu.VMEM((2, 2, T, HD), BF),
            pltpu.VMEM((2, 2, 2 * T, HD), BF),
            pltpu.VMEM((2, 2 * T, HD), BF),
            pltpu.VMEM((4, T, D), BF),
            pltpu.VMEM((4, T, D), BF),
            pltpu.VMEM((2, T // 2, D), BF),
            pltpu.VMEM((2, T, D), BF),
            pltpu.VMEM((4, T, D), BF),
            pltpu.SemaphoreType.DMA((sems,)),
            pltpu.SemaphoreType.DMA((sems,)),
            pltpu.SemaphoreType.DMA((7,)),
        ],
        compiler_params=pltpu.CompilerParams(
            collective_id=1, has_side_effects=True, vmem_limit_bytes=62 * 1024 * 1024),
        cost_estimate=pl.CostEstimate(flops=3_400_000_000, bytes_accessed=40_000_000, transcendentals=0),
    )(dk, dv, attn, wall, dq)


def hand_on_kernel(*refs):
    count = (len(refs) - 1) // 3
    sems = refs[-1]
    inward, outward = [], []
    for src, dst, held in zip(refs[:count], refs[count:2 * count], refs[2 * count:-1]):
        rows = src.shape[0] // 2
        for i in range(2):
            part = pl.ds(i * rows, rows)
            n = len(inward)
            inward.append(pltpu.make_async_copy(src.at[part, :], held.at[part, :], sems.at[0, n]))
            outward.append(pltpu.make_async_copy(held.at[part, :], dst.at[part, :], sems.at[1, n]))
            inward[-1].start()
    for first, second in zip(inward, outward):
        first.wait()
        second.start()
    for copy in outward:
        copy.wait()


def hand_on(*arrays):
    hbm = pl.BlockSpec(memory_space=pltpu.HBM)
    return pl.pallas_call(
        hand_on_kernel,
        out_shape=tuple(jax.ShapeDtypeStruct(a.shape, a.dtype) for a in arrays),
        in_specs=[hbm] * len(arrays),
        out_specs=(hbm,) * len(arrays),
        scratch_shapes=[pltpu.VMEM(a.shape, a.dtype) for a in arrays] + [
            pltpu.SemaphoreType.DMA((2, 2 * len(arrays)))],
        compiler_params=pltpu.CompilerParams(vmem_limit_bytes=62 * 1024 * 1024),
        cost_estimate=pl.CostEstimate(flops=0, bytes_accessed=5_000_000, transcendentals=0),
    )(*arrays)


def on_device(queries, keys, values, out_weight, d_proj, block_section, section_parent, xref_owner, xref_block, xref_valid):
    seq = lax.axis_size("seq")
    qh, kall, vall, wall, d_attn, *xrefs = gather(
        queries, keys, values, out_weight.T, d_proj, (xref_owner, xref_block, xref_valid), seq)
    attn, dq, dk, dv = attention(block_section, section_parent, xrefs, qh, kall, vall, d_attn)
    return hand_on(*scatter(dk, dv, attn, wall, dq, d_proj.shape[1]))


def solution(mesh):
    split = P("seq", "head")
    rows = P("seq", None)
    return jax.shard_map(
        on_device, mesh=mesh,
        in_specs=(split, split, split, P("head", "seq"), split, P(), P(), rows, rows, rows),
        out_specs=(split,) * 4, check_vma=False)
```

```python
import functools
import jax, jax.numpy as jnp
from jax import lax
from jax.experimental import pallas as pl
from jax.experimental.pallas import tpu as pltpu
from jax.sharding import PartitionSpec as P
F32, BF = jnp.float32, jnp.bfloat16
MESH = pl.DeviceIdType.MESH
RING = 4


HD = 128
BLK = 128
CHUNK = 4
BOTH = 2


def attention_kernel(NBLK, NSEC, NQ, G, XR, sec_hbm, par_hbm, xo_hbm, xb_hbm, xv_hbm, q_hbm, k_hbm, v_hbm, do_hbm, attn_hbm, dq_hbm, dk_hbm, dv_hbm,
                     kc, vc, ak, av, sbuf0, sbuf1, q_ref, do_ref, attn_ref, dq_ref, dk_ref, dv_ref,
                     qs_t, dot_t, ot0, ot1, shares, slots, counts, turn, first, stop, done, sec, parent, xo, xb, xv, sems):
    scaling = HD ** -0.5
    sbuf, ot = (sbuf0, sbuf1), (ot0, ot1)
    NT = (((1,), (1,)), ((), ()))
    TN = (((0,), (0,)), ((), ()))
    NN = (((1,), (0,)), ((), ()))
    R = CHUNK * BLK

    def mm(a, b, dims):
        return lax.dot_general(a, b, dims, preferred_element_type=F32)

    loads = [pltpu.make_async_copy(src, dst, sems.at[i]) for i, (src, dst) in enumerate((
        (k_hbm, kc.at[pl.ds(0, NBLK * BLK)]), (v_hbm, vc.at[pl.ds(0, NBLK * BLK)]), (q_hbm, q_ref), (do_hbm, do_ref)))]
    tables = [pltpu.make_async_copy(src, dst, sems.at[32 + i]) for i, (src, dst) in enumerate((
        (sec_hbm, sec), (par_hbm, parent), (xo_hbm, xo), (xb_hbm, xb), (xv_hbm, xv)))]
    for copy in tables + loads:
        copy.start()
    for copy in tables:
        copy.wait()
    begin = (lax.axis_index("seq") // 2) * NQ

    @pl.loop(0, NSEC)
    def _(s):
        stop[s] = 0
        first[s] = 0
        done[s] = 0

    @pl.loop(0, NBLK // 8)
    def _(i):
        for h in range(8):
            c = i * 8 + h
            stop[sec[c]] = c + 1
            d = NBLK - 1 - c
            first[sec[d]] = d

    @pl.loop(0, NQ)
    def _(b):
        g = begin + b
        mine = sec[g]
        for j in range(32):
            slots[b, j] = g
        slots[b, 1] = NBLK + mine
        n = jnp.int32(2)
        for w in (1, 2, 3):
            c = g - w
            cs = jnp.maximum(c, 0)
            slots[b, n] = cs
            n = n + jnp.where((c >= 0) & (sec[cs] == mine), 1, 0)
        up = parent[mine]
        slots[b, n] = NBLK + jnp.maximum(up, 0)
        n = n + jnp.where(up >= 0, 1, 0)
        core, row = lax.div(b, NQ // 2), lax.rem(b, NQ // 2)
        for j in range(XR):
            slots[b, n] = xo[core, 0, row * XR + j] * (NQ // 2) + xb[core, row, j] + 256
            n = n + jnp.where(xv[core, row, j] > 0, 1, 0)
        slots[b, n] = g
        counts[b] = n

    for b in range(NQ):
        place = jnp.int32(0)
        for o in range(NQ):
            if o < b:
                place = place + jnp.where(counts[o] >= counts[b], 1, 0)
            elif o > b:
                place = place + jnp.where(counts[o] > counts[b], 1, 0)
        turn[place] = b

    @pl.loop(0, (NBLK + NSEC) // 4)
    def _(i):
        at = pl.ds(pl.multiple_of(i * 512, 512), 512)
        ak[at, :] = jnp.zeros((512, HD), F32)
        av[at, :] = jnp.zeros((512, HD), F32)

    for copy in loads:
        copy.wait()

    def span(i):
        return pl.ds(pl.multiple_of(i * BLK, BLK), BLK)

    def summarize(s):
        def add(c, t):
            return t[0] + kc[span(c), :].astype(F32), t[1] + vc[span(c), :].astype(F32)
        zero = jnp.zeros((BLK, HD), F32)
        tk, tv = lax.fori_loop(first[s], stop[s], add, (zero, zero))
        share = 1.0 / jnp.sqrt(jnp.full((8, HD), jnp.maximum(stop[s] - first[s], 1)).astype(F32))
        shares[s] = share
        kc[span(NBLK + s), :] = (tk * share[:1]).astype(BF)
        vc[span(NBLK + s), :] = (tv * share[:1]).astype(BF)
        done[s] = 1

    @pl.loop(0, 2 * NQ)
    def _(i):
        mine = sec[begin + lax.div(i, 2)]
        s = jnp.where(lax.rem(i, 2) == 0, mine, jnp.maximum(parent[mine], 0))

        @pl.when(done[s] == 0)
        def _():
            summarize(s)

    W = G * BLK
    row_id = lax.broadcasted_iota(jnp.int32, (BLK, BLK), 0)
    col_id = lax.broadcasted_iota(jnp.int32, (BLK, BLK), 1)
    causal = jnp.concatenate([row_id <= col_id] * G, axis=1)

    def fold(op, s):
        return op(s.reshape(s.shape[0] // 8, 8, W), axis=0)

    ones = jnp.ones((R, 16), BF)

    TWO = range(BOTH)

    @pl.loop(0, NQ // BOTH)
    def _(u):
        bs = [turn[u * BOTH + t] for t in TWO]
        bases = [pl.multiple_of(b * BLK, BLK) for b in bs]
        for t in TWO:
            for g in range(G):
                part = slice(g * BLK, (g + 1) * BLK)
                qs_t[t, :, part] = q_ref[pl.ds(bases[t], BLK), part].astype(F32).T.astype(BF)
                dot_t[t, :, part] = do_ref[pl.ds(bases[t], BLK), part].astype(F32).T.astype(BF)
        ns = [counts[b] for b in bs]
        most = ns[0]
        for n in ns[1:]:
            most = jnp.maximum(most, n)
        chunks = lax.div(most + CHUNK - 1, CHUNK)

        def chunk(t, ref, j):
            return jnp.concatenate([ref[span(slots[bs[t], CHUNK * j + h] & 255), :] for h in range(CHUNK)], axis=0)

        def rows(j):
            return pl.ds(pl.multiple_of(j * R, R), R)

        def scores(t, j, full=False):
            s = mm(chunk(t, kc, j), qs_t[t], NN) * scaling
            if full:
                return s
            return jnp.concatenate([
                s[h * BLK:(h + 1) * BLK] + jnp.where(CHUNK * j + h < ns[t], 0.0, -1e30) for h in range(CHUNK)], axis=0)

        tops = []
        for t in TWO:
            s0 = scores(t, 0)
            s0 = jnp.concatenate([jnp.where(causal, s0[:BLK], -1e30), s0[BLK:]], axis=0)
            sbuf[t][rows(0), :] = s0
            tops.append(fold(jnp.max, s0))

        def score(full, j, ms):
            ss = [scores(t, j, full) for t in TWO]
            for t in TWO:
                sbuf[t][rows(j), :] = ss[t]
            return tuple(jnp.maximum(ms[t], fold(jnp.max, ss[t])) for t in TWO)
        fewest = ns[0]
        for n in ns[1:]:
            fewest = jnp.minimum(fewest, n)
        whole = jnp.maximum(lax.div(fewest, CHUNK), 1)
        tops = lax.fori_loop(1, whole, functools.partial(score, True), tuple(tops))
        tops = lax.fori_loop(whole, chunks, functools.partial(score, False), tops)
        tops = [jnp.max(m, axis=0, keepdims=True) for m in tops]

        for t in TWO:
            ot[t][...] = jnp.zeros((HD + 16, W), F32)

        def forward(j, carry):
            es = [jnp.exp(sbuf[t][rows(j), :] - tops[t]) for t in TWO]
            for t in TWO:
                sbuf[t][rows(j), :] = es[t]
            for t in TWO:
                ot[t][...] += mm(jnp.concatenate([chunk(t, vc, j), ones], axis=1), es[t].astype(BF), TN)
            return carry
        lax.fori_loop(0, chunks, forward, 0)
        rls, deltas = [], []
        for t in TWO:
            rl = 1.0 / ot[t][HD:HD + 1, :]
            o_t = (ot[t][:HD, :] * rl).astype(BF).astype(F32)
            rls.append(rl)
            deltas.append(jnp.sum(o_t * dot_t[t].astype(F32), axis=0, keepdims=True))
            for g in range(G):
                part = slice(g * BLK, (g + 1) * BLK)
                attn_ref[pl.ds(bases[t], BLK), part] = o_t[:, part].T.astype(BF)

        def put(acc, t, i, term):
            slot = slots[bs[t], i]
            where = span(slot & 255)
            acc[where, :] += jnp.where(slot >= 256, term.astype(BF).astype(F32), term)

        for t in TWO:
            ot[t][:HD, :] = jnp.zeros((HD, W), F32)

        def backward(j, carry):
            terms = []
            for t in TWO:
                k, v = chunk(t, kc, j), chunk(t, vc, j)
                p = sbuf[t][rows(j), :] * rls[t]
                ds = (p * (mm(v, dot_t[t], NN) - deltas[t])).astype(BF)
                dv = mm(dot_t[t], p.astype(BF), NT)
                dk = mm(qs_t[t], ds, NT) * scaling
                ot[t][:HD, :] += mm(k, ds, TN)
                terms.append((dk, dv))
            for t in TWO:
                dk, dv = terms[t]
                for h in range(CHUNK):
                    put(ak, t, CHUNK * j + h, dk[:, h * BLK:(h + 1) * BLK])
                    put(av, t, CHUNK * j + h, dv[:, h * BLK:(h + 1) * BLK])
            return carry
        lax.fori_loop(0, chunks, backward, 0)
        for t in TWO:
            for g in range(G):
                part = slice(g * BLK, (g + 1) * BLK)
                dq_ref[pl.ds(bases[t], BLK), part] = (ot[t][:HD, part] * scaling).T.astype(BF)

    saves = [pltpu.make_async_copy(attn_ref, attn_hbm, sems.at[4]), pltpu.make_async_copy(dq_ref, dq_hbm, sems.at[5])]
    for copy in saves:
        copy.start()
    @pl.loop(0, NSEC)
    def _(s):
        @pl.when(done[s] == 1)
        def _():
            share = shares[s][:1]
            gk, gv = ak[span(NBLK + s), :] * share, av[span(NBLK + s), :] * share

            @pl.loop(first[s], stop[s])
            def _(c):
                ak[span(c), :] += gk
                av[span(c), :] += gv

    STEP = 4
    PARTS = 8

    for part in range(PARTS):
        size = NBLK // PARTS

        @pl.loop(part * size // STEP, (part + 1) * size // STEP)
        def _(i):
            at = pl.ds(pl.multiple_of(i * STEP * BLK, STEP * BLK), STEP * BLK)
            dk_ref[at, :] = ak[at, :].astype(BF)
            dv_ref[at, :] = av[at, :].astype(BF)
        at = pl.ds(part * size * BLK, size * BLK)
        for j, (src, dst) in enumerate(((dk_ref, dk_hbm), (dv_ref, dv_hbm))):
            copy = pltpu.make_async_copy(src.at[at, :], dst.at[at, :], sems.at[6 + 2 * part + j])
            copy.start()
            saves.append(copy)
    for copy in saves:
        copy.wait()


def attention(block_section, section_parent, xrefs, q, k, v, do):
    NSEC = section_parent.shape[0]
    XR = xrefs[1].shape[2]
    NBLK = k.shape[0] // BLK
    NQ = q.shape[0] // BLK
    G = q.shape[1] // HD
    W = G * BLK
    slots_most = -(-(6 + XR) // CHUNK) * CHUNK
    hbm = pl.BlockSpec(memory_space=pltpu.HBM)
    every = ((NBLK + NSEC) * BLK, HD)
    return pl.pallas_call(
        functools.partial(attention_kernel, NBLK, NSEC, NQ, G, XR),
        out_shape=(jax.ShapeDtypeStruct(q.shape, BF), jax.ShapeDtypeStruct(q.shape, BF),
                   jax.ShapeDtypeStruct(k.shape, BF), jax.ShapeDtypeStruct(k.shape, BF)),
        in_specs=[hbm] * 9,
        out_specs=(hbm,) * 4,
        scratch_shapes=[
            pltpu.VMEM(every, BF),
            pltpu.VMEM(every, BF),
            pltpu.VMEM(every, F32),
            pltpu.VMEM(every, F32),
            pltpu.VMEM((slots_most * BLK, W), F32),
            pltpu.VMEM((slots_most * BLK, W), F32),
            pltpu.VMEM(q.shape, BF),
            pltpu.VMEM(q.shape, BF),
            pltpu.VMEM(q.shape, BF),
            pltpu.VMEM(q.shape, BF),
            pltpu.VMEM(k.shape, BF),
            pltpu.VMEM(k.shape, BF),
            pltpu.VMEM((BOTH, HD, W), BF),
            pltpu.VMEM((BOTH, HD, W), BF),
            pltpu.VMEM((HD + 16, W), F32),
            pltpu.VMEM((HD + 16, W), F32),
            pltpu.VMEM((NSEC, 8, HD), F32),
            pltpu.SMEM((NQ, 32), jnp.int32),
            pltpu.SMEM((NQ,), jnp.int32),
            pltpu.SMEM((NQ,), jnp.int32),
            pltpu.SMEM((NSEC,), jnp.int32),
            pltpu.SMEM((NSEC,), jnp.int32),
            pltpu.SMEM((NSEC,), jnp.int32),
            pltpu.SMEM(block_section.shape, jnp.int32),
            pltpu.SMEM(section_parent.shape, jnp.int32),
        ] + [pltpu.SMEM(a.shape, jnp.int32) for a in xrefs] + [
            pltpu.SemaphoreType.DMA((40,)),
        ],
        compiler_params=pltpu.CompilerParams(vmem_limit_bytes=62 * 1024 * 1024),
        cost_estimate=pl.CostEstimate(flops=18_000_000_000, bytes_accessed=24_000_000, transcendentals=12_000_000),
    )(block_section, section_parent, *xrefs, q, k, v, do)


class Links:
    def __init__(self, send_sems, recv_sems):
        s = lax.axis_index("seq")
        self.y = lax.axis_index("head")
        self.x = s // 8
        self.z = (s // 2) % RING
        self.c = s % 2
        self.send_sems, self.recv_sems = send_sems, recv_sems
        self.used = 0
        self.sent = []

    def device(self, axis, step):
        x, z, y, c = self.x, self.z, self.y, self.c
        if axis == "x":
            x = (x + step) % RING
        elif axis == "z":
            z = (z + step) % RING
        elif axis == "y":
            y = (y + step) % RING
        else:
            c = 1 - c
        return ((x * RING + z) * 2 + c, y)

    def everyone(self):
        return [self.device(a, d) for a in "xzy" for d in (1, RING - 1)] + [self.device("c", 1)]

    def barrier(self):
        sem = pltpu.get_barrier_semaphore()
        for device in self.everyone():
            pl.semaphore_signal(sem, inc=1, device_id=device, device_id_type=MESH)
        pl.semaphore_wait(sem, 7)

    def number(self):
        self.used += 1
        return self.used - 1

    def send(self, number, src, dst, axis, step):
        copy = pltpu.make_async_remote_copy(
            src_ref=src, dst_ref=dst, send_sem=self.send_sems.at[number], recv_sem=self.recv_sems.at[number],
            device_id=self.device(axis, step), device_id_type=MESH)
        copy.start()
        self.sent.append(copy)

    def arrived(self, number, dst):
        pltpu.make_async_remote_copy(
            src_ref=dst, dst_ref=dst, send_sem=self.send_sems.at[number], recv_sem=self.recv_sems.at[number],
            device_id=self.device("c", 1), device_id_type=MESH).wait_recv()

    def finish(self):
        for copy in self.sent:
            copy.wait_send()


class Gather:
    def __init__(self, links, array, rows, pitch, offset, split, a, b):
        self.L, self.array, self.rows, self.pitch, self.offset, self.split = links, array, rows, pitch, offset, split
        self.a, self.b = a, b
        self.na = [links.number() for _ in range(4)]
        self.nb = [[links.number() for _ in range(4)] for _ in range(4)]

    def at(self, da, db, half=None):
        L = self.L
        move = {self.a: da, self.b: db}
        x, z = (L.x + move["x"]) % RING, (L.z + move["z"]) % RING
        start, count = self.offset, self.rows
        if half == 0:
            count = self.split
        elif half == 1:
            start, count = self.offset + self.split, self.rows - self.split
        return self.array.at[pl.ds(pl.multiple_of((x * RING + z) * self.pitch + start, 16), count), :]

    def put(self, number, axis, step, da, db, half=None):
        self.L.send(number, self.at(da, db, half), self.at(da, db, half), axis, step)

    def begin(self):
        self.put(self.na[0], self.a, 1, 0, 0)
        self.put(self.na[1], self.a, 3, 0, 0)

    def spread(self, i, da):
        self.put(self.nb[i][0], self.b, 1, da, 0)
        self.put(self.nb[i][1], self.b, 3, da, 0)

    def near(self):
        self.L.arrived(self.na[0], self.at(3, 0))
        self.put(self.na[2], self.a, 1, 3, 0, 0)
        self.L.arrived(self.na[1], self.at(1, 0))
        self.put(self.na[3], self.a, 3, 1, 0, 1)
        self.spread(0, 0)
        self.spread(1, 3)
        self.spread(2, 1)

    def far(self):
        self.L.arrived(self.na[2], self.at(2, 0, 0))
        self.L.arrived(self.na[3], self.at(2, 0, 1))
        self.spread(3, 2)

    def relay(self, i):
        da = (0, 3, 1, 2)[i]
        self.L.arrived(self.nb[i][0], self.at(da, 3))
        self.put(self.nb[i][2], self.b, 1, da, 3, 0)
        self.L.arrived(self.nb[i][1], self.at(da, 1))
        self.put(self.nb[i][3], self.b, 3, da, 1, 1)

    def end(self, i):
        da = (0, 3, 1, 2)[i]
        self.L.arrived(self.nb[i][2], self.at(da, 2, 0))
        self.L.arrived(self.nb[i][3], self.at(da, 2, 1))


def gather_kernel(q_hbm, k_hbm, v_hbm, wt_hbm, dp_hbm, xo, xb, xv, qh, kall, vall, wall, dattn, xos, xbs, xvs, q, k, v, wt, dp, wbuf, dbuf, abuf, send_sems, recv_sems, own_sems):
    L = Links(send_sems, recv_sems)
    chip = L.x * RING + L.z
    other = 1 - L.c
    T = k.shape[0]
    HD = kall.shape[1]
    W = qh.shape[1]
    C = wt.shape[0]
    D = dp.shape[1]
    loads = [pltpu.make_async_copy(src, dst, own_sems.at[11 + i]) for i, (src, dst) in enumerate((
        (wt_hbm, wt), (k_hbm, k), (v_hbm, v), (dp_hbm, dp), (q_hbm, q)))]
    for copy in loads:
        copy.start()
    L.barrier()
    for copy in loads:
        copy.wait()

    pairs = []

    def split(src, width, dst, first, rows):
        at = dst.at[pl.ds(pl.multiple_of(first, 16), rows), :]
        pairs.append((L.number(), src, width, dst, at, rows))

    mine = chip * 2 * T + L.c * T
    split(wt, W, wbuf, chip * 2 * C + L.c * C, C)
    split(k, HD, kall, mine, T)
    split(v, HD, vall, mine, T)
    split(q, W, qh, L.c * T, T)
    own = []
    for i, (number, src, width, dst, at, rows) in enumerate(pairs):
        L.send(number, src.at[:, pl.ds(pl.multiple_of(other * width, 128), width)], at, "c", 1)
        copy = pltpu.make_async_copy(src.at[:, pl.ds(pl.multiple_of(L.c * width, 128), width)], at, own_sems.at[i])
        copy.start()
        own.append(copy)
    refs = []
    for i, (src, dst) in enumerate(((xo, xos), (xb, xbs), (xv, xvs))):
        n = L.number()
        L.send(n, src, dst.at[L.c], "c", 1)
        copy = pltpu.make_async_copy(src, dst.at[L.c], own_sems.at[8 + i])
        copy.start()
        refs.append((n, dst, copy))

    def piece(core, dy, half=None):
        ref = dbuf.at[core * RING + (L.y + dy) % RING]
        if half is None:
            return ref
        return ref.at[pl.ds(half * (T // 2), T // 2), :]

    ny = [L.number() for _ in range(4)]
    nc = [L.number() for _ in range(4)]
    L.send(ny[0], dp, piece(L.c, 0), "y", 1)
    L.send(ny[1], dp, piece(L.c, 0), "y", 3)
    L.send(nc[0], dp, piece(L.c, 0), "c", 1)
    own_d = pltpu.make_async_copy(dp, piece(L.c, 0), own_sems.at[5])
    own_d.start()

    sibling = [chip * 2 * C + other * C, chip * 2 * T + other * T, chip * 2 * T + other * T, other * T]

    def both(i):
        number, src, width, dst, at, rows = pairs[i]
        L.arrived(number, dst.at[pl.ds(pl.multiple_of(sibling[i], 16), rows), :])
        own[i].wait()

    first_w = (C // 2 + 15) // 16 * 16
    w0 = Gather(L, wbuf, C, 2 * C, 0, first_w, "x", "z")
    w1 = Gather(L, wbuf, C, 2 * C, C, first_w, "z", "x")
    gk = Gather(L, kall, 2 * T, 2 * T, 0, T, "x", "z")
    gv = Gather(L, vall, 2 * T, 2 * T, 0, T, "z", "x")
    both(0)
    w0.begin()
    w1.begin()
    both(1)
    gk.begin()
    both(2)
    gv.begin()
    w0.near()
    w1.near()
    gk.near()
    gv.near()
    w0.far()
    w1.far()
    gk.far()
    gv.far()
    L.arrived(ny[0], piece(L.c, 3))
    L.send(ny[2], piece(L.c, 3, 0), piece(L.c, 3, 0), "y", 1)
    L.arrived(ny[1], piece(L.c, 1))
    L.send(ny[3], piece(L.c, 1, 1), piece(L.c, 1, 1), "y", 3)
    L.send(nc[1], piece(L.c, 3), piece(L.c, 3), "c", 1)
    L.send(nc[2], piece(L.c, 1), piece(L.c, 1), "c", 1)
    for i in range(4):
        w0.relay(i)
        w1.relay(i)
    for i in range(2):
        gk.relay(i)
        gv.relay(i)
    L.arrived(ny[2], piece(L.c, 2, 0))
    L.arrived(ny[3], piece(L.c, 2, 1))
    L.send(nc[3], piece(L.c, 2), piece(L.c, 2), "c", 1)
    for i in range(4):
        w0.end(i)
        w1.end(i)
    keep = pltpu.make_async_copy(wbuf, wall, own_sems.at[6])
    keep.start()

    step = 256

    def product(core, t):
        rows = pl.ds(pl.multiple_of(t * step, step), step)
        total = jnp.zeros((step, W), F32)
        for y in range(RING):
            total += jnp.dot(dbuf[core * RING + y, rows, :], wbuf[y * D:(y + 1) * D, :], preferred_element_type=F32)
        abuf[pl.ds(pl.multiple_of(core * T + t * step, step), step), :] = total.astype(BF)

    def products(core):
        @pl.loop(0, T // step)
        def _(t):
            product(core, t)

    gk.relay(2)
    gv.relay(2)
    own_d.wait()
    products(L.c)
    gk.relay(3)
    gv.relay(3)
    for i, dy in enumerate((0, 3, 1, 2)):
        L.arrived(nc[i], piece(other, dy))
    products(other)
    save = pltpu.make_async_copy(abuf, dattn, own_sems.at[7])
    save.start()
    for i in range(4):
        gk.end(i)
        gv.end(i)
    both(3)
    for n, dst, copy in refs:
        L.arrived(n, dst.at[other])
        copy.wait()
    keep.wait()
    save.wait()
    L.finish()


def gather(q, k, v, wt, dp, xrefs, seq):
    T = k.shape[0]
    HD = k.shape[1] // 2
    W = q.shape[1] // 2
    C = wt.shape[0]
    D = dp.shape[1]
    anywhere = pl.BlockSpec(memory_space=pltpu.HBM)
    sems = 128
    return pl.pallas_call(
        gather_kernel,
        out_shape=(
            jax.ShapeDtypeStruct((2 * T, W), BF),
            jax.ShapeDtypeStruct((seq * T, HD), BF),
            jax.ShapeDtypeStruct((seq * T, HD), BF),
            jax.ShapeDtypeStruct((seq * C, W), BF),
            jax.ShapeDtypeStruct((2 * T, W), BF),
        ) + tuple(jax.ShapeDtypeStruct((2,) + a.shape, jnp.int32) for a in xrefs),
        in_specs=[anywhere] * 8,
        out_specs=(anywhere,) * 8,
        scratch_shapes=[pltpu.VMEM(a.shape, BF) for a in (q, k, v, wt, dp)] + [
            pltpu.VMEM((seq * C, W), BF),
            pltpu.VMEM((2 * RING, T, D), BF),
            pltpu.VMEM((2 * T, W), BF),
            pltpu.SemaphoreType.DMA((sems,)),
            pltpu.SemaphoreType.DMA((sems,)),
            pltpu.SemaphoreType.DMA((16,)),
        ],
        compiler_params=pltpu.CompilerParams(
            collective_id=0, has_side_effects=True, vmem_limit_bytes=62 * 1024 * 1024),
        cost_estimate=pl.CostEstimate(flops=3_400_000_000, bytes_accessed=40_000_000, transcendentals=0),
    )(q, k, v, wt, dp, *xrefs)


class Scatter:
    def __init__(self, links, source, buf, far, near, far2, near2, final, a, b, load_sem):
        self.L, self.source, self.buf = links, source, buf
        self.farr, self.nearr, self.far2, self.near2, self.final = far, near, far2, near2, final
        self.a, self.b = a, b
        self.rows = final.shape[0]
        self.nb = [[links.number() for _ in range(4)] for _ in range(4)]
        self.na = [links.number() for _ in range(4)]
        self.load = pltpu.make_async_copy(source, buf, load_sem)
        self.load.start()

    def where(self, da, db, half=None):
        L = self.L
        move = {self.a: da, self.b: db}
        x, z = (L.x + move["x"]) % RING, (L.z + move["z"]) % RING
        start, count = 0, self.rows
        if half is not None:
            count = self.rows // 2
            start = half * count
        return pl.ds(pl.multiple_of((x * RING + z) * self.rows + start, 16), count)

    def half(self, h):
        return pl.ds(h * (self.rows // 2), self.rows // 2)

    def begin(self, i):
        da = (2, 3, 1, 0)[i]
        for h, step in ((0, 1), (1, 3)):
            self.L.send(self.nb[i][h], self.source.at[self.where(da, 2, h), :], self.farr.at[i, h], self.b, step)

    def loaded(self):
        self.load.wait()

    def pass_on(self, i):
        da = (2, 3, 1, 0)[i]
        for h, step in ((0, 1), (1, 3)):
            self.L.arrived(self.nb[i][h], self.farr.at[i, h])
            at = self.where(da, step, h)
            self.buf[at, :] = (self.buf[at, :].astype(F32) + self.farr[i, h].astype(F32)).astype(BF)
            self.L.send(self.nb[i][2 + h], self.buf.at[self.where(da, step), :], self.nearr.at[i, h], self.b, step)

    def total(self, i, da, h):
        at = self.where(da, 0, h)
        part = self.half(h)
        return (self.buf[at, :].astype(F32) + self.nearr[i, 0, part, :].astype(F32)
                + self.nearr[i, 1, part, :].astype(F32))

    def close(self, i):
        da = (2, 3, 1, 0)[i]
        for h in range(2):
            self.L.arrived(self.nb[i][2 + h], self.nearr.at[i, h])
        if i == 0:
            for h, step in ((0, 1), (1, 3)):
                at = self.where(da, 0, h)
                self.buf[at, :] = self.total(i, da, h).astype(BF)
                self.L.send(self.na[h], self.buf.at[at, :], self.far2.at[h], self.a, step)
        elif i < 3:
            take = 1 if da == 3 else 0
            self.L.arrived(self.na[take], self.far2.at[take])
            for h in range(2):
                value = self.total(i, da, h)
                if h == take:
                    value += self.far2[take].astype(F32)
                self.buf[self.where(da, 0, h), :] = value.astype(BF)
            self.L.send(self.na[2 + take], self.buf.at[self.where(da, 0), :], self.near2.at[take], self.a, da)

    def finish(self):
        for take in range(2):
            self.L.arrived(self.na[2 + take], self.near2.at[take])
        for h in range(2):
            part = self.half(h)
            value = (self.total(3, 0, h) + self.near2[0, part, :].astype(F32)
                     + self.near2[1, part, :].astype(F32))
            self.final[part, :] = jnp.concatenate(
                [value[i:i + BLK].T for i in range(0, value.shape[0], BLK)], axis=0).astype(BF)


def scatter_kernel(dk, dv, attn, wall, dq_hbm, proj, dqo, dko, dvo,
                   dq, bufk, bufv, farr, nearr, far2, near2, final, there, here, halves, wholes, result,
                   send_sems, recv_sems, own_sems):
    L = Links(send_sems, recv_sems)
    other = 1 - L.c
    T = proj.shape[0]
    D = proj.shape[1]
    W = dq.shape[1]
    HD = dk.shape[1]
    load_q = pltpu.make_async_copy(dq_hbm, dq, own_sems.at[6])
    load_q.start()
    L.barrier()
    sk = Scatter(L, dk, bufk, farr.at[0], nearr.at[0], far2.at[0], near2.at[0], final.at[0], "x", "z", own_sems.at[0])
    sv = Scatter(L, dv, bufv, farr.at[1], nearr.at[1], far2.at[1], near2.at[1], final.at[1], "z", "x", own_sems.at[1])
    for i in range(2):
        sk.begin(i)
        sv.begin(i)

    def rows_of(core):
        return pl.ds(pl.multiple_of(core * T, 16), T)

    def heads(ref, core, width):
        return ref.at[:, pl.ds(pl.multiple_of(core * width, 128), width)]

    load_q.wait()
    n_q = L.number()
    L.send(n_q, dq.at[rows_of(other), :], heads(dqo, L.c, W), "c", 1)
    own_q = pltpu.make_async_copy(dq.at[rows_of(L.c), :], heads(dqo, L.c, W), own_sems.at[2])
    own_q.start()

    n_there = [L.number() for _ in range(4)]
    ny = [L.number() for _ in range(4)]
    order = (2, 1, 3, 0)

    def product(core, dy):
        y = (L.y + dy) % RING
        w = wall[pl.ds(pl.multiple_of(y * D, 16), D), :]
        return lax.dot_general(attn[rows_of(core), :], w, (((1,), (1,)), ((), ())), preferred_element_type=F32)

    def away(i):
        here[i] = product(other, order[i]).astype(BF)
        L.send(n_there[i], here.at[i], there.at[i], "c", 1)

    def mine(i):
        value = product(L.c, order[i])
        L.arrived(n_there[i], there.at[i])
        return value + there[i].astype(F32)

    mid = T // 2
    away(0)
    sk.loaded()
    sv.loaded()
    sk.pass_on(0)
    sv.pass_on(0)
    sk.begin(2)
    sv.begin(2)
    away(1)
    sk.pass_on(1)
    sv.pass_on(1)
    sk.begin(3)
    sv.begin(3)
    away(2)
    sk.close(0)
    sv.close(0)
    away(3)
    sk.pass_on(2)
    sv.pass_on(2)
    result[0] = mine(0).astype(BF)
    L.send(ny[0], result.at[0, pl.ds(0, mid), :], halves.at[0], "y", 1)
    L.send(ny[1], result.at[0, pl.ds(mid, mid), :], halves.at[1], "y", 3)
    sk.close(1)
    sv.close(1)
    sk.pass_on(3)
    sv.pass_on(3)
    value = mine(1)
    L.arrived(ny[0], halves.at[0])
    result[1] = jnp.concatenate([value[:mid] + halves[0].astype(F32), value[mid:]], axis=0).astype(BF)
    L.send(ny[2], result.at[1], wholes.at[0], "y", 1)
    value = mine(2)
    L.arrived(ny[1], halves.at[1])
    result[2] = jnp.concatenate([value[:mid], value[mid:] + halves[1].astype(F32)], axis=0).astype(BF)
    L.send(ny[3], result.at[2], wholes.at[1], "y", 3)
    sk.close(2)
    sv.close(2)
    value = mine(3)
    L.arrived(ny[2], wholes.at[0])
    L.arrived(ny[3], wholes.at[1])
    result[3] = (value + wholes[0].astype(F32) + wholes[1].astype(F32)).astype(BF)
    own_p = pltpu.make_async_copy(result.at[3], proj, own_sems.at[3])
    own_p.start()
    outs = []
    for j, (s, out) in enumerate(((sk, dko), (sv, dvo))):
        s.close(3)
        s.finish()
        n = L.number()
        L.send(n, final.at[j, rows_of(other), :], heads(out, L.c, HD), "c", 1)
        own = pltpu.make_async_copy(final.at[j, rows_of(L.c), :], heads(out, L.c, HD), own_sems.at[4 + j])
        own.start()
        outs.append((n, out, own))
    L.arrived(n_q, heads(dqo, other, W))
    own_q.wait()
    own_p.wait()
    for n, out, own in outs:
        L.arrived(n, heads(out, other, HD))
        own.wait()
    L.finish()


def scatter(dk, dv, attn, wall, dq, D):
    T = dq.shape[0] // 2
    W = dq.shape[1]
    HD = dk.shape[1]
    anywhere = pl.BlockSpec(memory_space=pltpu.HBM)
    vmem = pl.BlockSpec(memory_space=pltpu.VMEM)
    sems = 64
    return pl.pallas_call(
        scatter_kernel,
        out_shape=(
            jax.ShapeDtypeStruct((T, D), BF),
            jax.ShapeDtypeStruct((T, 2 * W), BF),
            jax.ShapeDtypeStruct((T, 2 * HD), BF),
            jax.ShapeDtypeStruct((T, 2 * HD), BF),
        ),
        in_specs=[anywhere, anywhere, vmem, vmem, anywhere],
        out_specs=(anywhere,) * 4,
        scratch_shapes=[
            pltpu.VMEM(dq.shape, BF),
            pltpu.VMEM(dk.shape, BF),
            pltpu.VMEM(dk.shape, BF),
            pltpu.VMEM((2, 4, 2, T, HD), BF),
            pltpu.VMEM((2, 4, 2, 2 * T, HD), BF),
            pltpu.VMEM((2, 2, T, HD), BF),
            pltpu.VMEM((2, 2, 2 * T, HD), BF),
            pltpu.VMEM((2, 2 * T, HD), BF),
            pltpu.VMEM((4, T, D), BF),
            pltpu.VMEM((4, T, D), BF),
            pltpu.VMEM((2, T // 2, D), BF),
            pltpu.VMEM((2, T, D), BF),
            pltpu.VMEM((4, T, D), BF),
            pltpu.SemaphoreType.DMA((sems,)),
            pltpu.SemaphoreType.DMA((sems,)),
            pltpu.SemaphoreType.DMA((7,)),
        ],
        compiler_params=pltpu.CompilerParams(
            collective_id=1, has_side_effects=True, vmem_limit_bytes=62 * 1024 * 1024),
        cost_estimate=pl.CostEstimate(flops=3_400_000_000, bytes_accessed=40_000_000, transcendentals=0),
    )(dk, dv, attn, wall, dq)


def hand_on_kernel(*refs):
    count = (len(refs) - 1) // 3
    sems = refs[-1]
    inward, outward = [], []
    for src, dst, held in zip(refs[:count], refs[count:2 * count], refs[2 * count:-1]):
        rows = src.shape[0] // 2
        for i in range(2):
            part = pl.ds(i * rows, rows)
            n = len(inward)
            inward.append(pltpu.make_async_copy(src.at[part, :], held.at[part, :], sems.at[0, n]))
            outward.append(pltpu.make_async_copy(held.at[part, :], dst.at[part, :], sems.at[1, n]))
            inward[-1].start()
    for first, second in zip(inward, outward):
        first.wait()
        second.start()
    for copy in outward:
        copy.wait()


def hand_on(*arrays):
    hbm = pl.BlockSpec(memory_space=pltpu.HBM)
    return pl.pallas_call(
        hand_on_kernel,
        out_shape=tuple(jax.ShapeDtypeStruct(a.shape, a.dtype) for a in arrays),
        in_specs=[hbm] * len(arrays),
        out_specs=(hbm,) * len(arrays),
        scratch_shapes=[pltpu.VMEM(a.shape, a.dtype) for a in arrays] + [
            pltpu.SemaphoreType.DMA((2, 2 * len(arrays)))],
        compiler_params=pltpu.CompilerParams(vmem_limit_bytes=62 * 1024 * 1024),
        cost_estimate=pl.CostEstimate(flops=0, bytes_accessed=5_000_000, transcendentals=0),
    )(*arrays)


def on_device(queries, keys, values, out_weight, d_proj, block_section, section_parent, xref_owner, xref_block, xref_valid):
    seq = lax.axis_size("seq")
    qh, kall, vall, wall, d_attn, *xrefs = gather(
        queries, keys, values, out_weight.T, d_proj, (xref_owner.T, xref_block, xref_valid), seq)
    attn, dq, dk, dv = attention(block_section, section_parent, xrefs, qh, kall, vall, d_attn)
    return hand_on(*scatter(dk, dv, attn, wall, dq, d_proj.shape[1]))


def solution(mesh):
    split = P("seq", "head")
    rows = P("seq", None)
    return jax.shard_map(
        on_device, mesh=mesh,
        in_specs=(split, split, split, P("head", "seq"), split, P(), P(), rows, rows, rows),
        out_specs=(split,) * 4, check_vma=False)
```
